256 devices in a mesh: ctx: 16 (over z, x_lo), ep: 16 (over y, x_hi, core).
Axes of the slice: x: 4 (x_hi: 2, x_lo: 2; x = x_hi * 2 + x_lo), y: 4, z: 8, core: 2. Of those that a mesh axis runs over, the one named last changes fastest.
Arguments:
- queries: bfloat16 [8192, 2048], P('ctx', 'ep'), may hold values from -8 to 8
- keys: bfloat16 [8192, 2048], P('ctx', 'ep'), may hold values from -8 to 8
- values: bfloat16 [8192, 2048], P('ctx', 'ep'), may hold values from -6 to 6
- segments: int32 [8192], replicated, may hold values from 0 to 2, as said below
- residual: bfloat16 [8192, 2048], P(('ctx', 'ep')), may hold values from -6 to 6
- out_weight: bfloat16 [2048, 2048], P('ep'), may hold values from -0.125 to 0.125
- norm_gain: float32 [2048], replicated, may hold values from 0.1 to 1.9
- router: float32 [2048, 64], replicated, may hold values from -0.125 to 0.125
- routes: int32 [8192, 6], P(('ctx', 'ep')), may hold values from 0 to 63, all different within a row; in each aligned block of 32 rows (0 to 31, 32 to 63, ...) at most 6 rows name the same one
- gate_weight: bfloat16 [16, 16, 2048, 352], P('ep', 'ctx'), may hold values from -0.125 to 0.125
- up_weight: bfloat16 [16, 16, 2048, 352], P('ep', 'ctx'), may hold values from -0.125 to 0.125
- down_weight: bfloat16 [16, 16, 352, 2048], P('ep', 'ctx'), may hold values from -0.15625 to 0.15625
Outputs:
- layer_out: bfloat16 [8192, 2048], P(('ctx', 'ep'))
The draws below stay inside these ranges and needn't reach their ends.
Inputs may be any that keep to these rules, and one draw needn't show every extreme that they name: In each aligned block of 32 rows (the rows of one device), no expert is named by more than 6 routes; each row names 6 different experts. `segments`: segment ids start at 0 and never fall along the window.
All inputs are finite; a program needn't handle non-finite values.
Results may differ from the reference program's by a relative error of at most 0.0075.
Values may be sent and summed in bfloat16 or wider, within the bound.
A program may use at most 128 MiB of HBM per device.

```python
import math
import jax
import jax.numpy as jnp
import numpy as np
from jax import lax

D = 2048
H = 16
HD = 128
FF = 1408
TOPK = 6
SPLIT = 4
SEQ = 8192
TOK = 32
EXPERTS = 64
FFQ = 352
CAP = 6
N_CTX = 16
N_EP = 16


def base_noise(key):
    return jnp.clip(1.5 * jax.random.normal(key, (SEQ, H * HD)), -6.0, 6.0)


def draw_queries(key, part):
    noise = base_noise(jax.random.fold_in(key, 1))
    return noise.astype(jnp.bfloat16)


def draw_keys(key, part):
    noise = base_noise(jax.random.fold_in(key, 2))
    return noise.astype(jnp.bfloat16)


def draw_segments(key, part):
    lower = jax.random.randint(jax.random.fold_in(key, 21), (), 1, SEQ // 4)
    upper = SEQ - jax.random.randint(jax.random.fold_in(key, 22), (), 1, SEQ // 4)
    positions = jnp.arange(SEQ, dtype=jnp.int32)
    return ((positions >= lower).astype(jnp.int32) + (positions >= upper).astype(jnp.int32)).astype(jnp.int32)


def levels(key, extent, cuts, low, largest):
    def one(dim, blocks):
        heights = jax.random.uniform(jax.random.fold_in(jax.random.fold_in(key, 6), dim), (blocks,), jnp.float32, low / len(cuts), largest / len(cuts))
        return jnp.repeat(jnp.exp(heights), extent[dim] // blocks).reshape((-1,) + (1,) * (len(extent) - dim - 1))

    factor_of = one(*cuts[0])
    for cut in cuts[1:]:
        factor_of = factor_of * one(*cut)
    return factor_of


def deal_out(key, own, number, rows, number_of, top, most, slope):
    ranking = jax.random.permutation(key, number_of)
    crowded, common = shares(number_of, rows * top, most, slope, True), shares(number_of, rows * top, most, slope, False)
    places = jnp.arange(number_of)

    def named(tallies, turn):
        used = int((tallies > 0).sum())
        fixed = max(1, used // 4)
        shifted = fixed + (places - fixed + turn * (used - fixed)) % max(1, number_of - fixed)
        return jnp.zeros((number_of,), jnp.int32).at[ranking[jnp.where(places < fixed, places, shifted)]].set(jnp.asarray(tallies, jnp.int32))

    tallies = jnp.where(number % 4 == 0, named(crowded, number // 4), named(common, number - number // 4 - 1))
    mixed = jax.random.permutation(jax.random.fold_in(own, 3), number_of)
    source_of, receiver = mixed[0:number_of // 2 * 2:2], mixed[1:number_of // 2 * 2:2]
    slack = jnp.minimum(tallies[source_of] - 1, most - tallies[receiver]) // 2
    slack = jnp.where((source_of == ranking[0]) | (receiver == ranking[0]) | (tallies[receiver] == 0), 0, jnp.maximum(slack, 0))
    shifted = jax.random.randint(jax.random.fold_in(own, 4), (number_of // 2,), 0, 1 << 20) % (slack + 1)
    tallies = tallies.at[source_of].add(-shifted).at[receiver].add(shifted)
    items = jnp.searchsorted(jnp.cumsum(tallies), jnp.arange(rows * top), side="right").astype(jnp.int32)
    table = items.reshape(top, rows).T
    table = table[jax.random.permutation(jax.random.fold_in(own, 1), rows)]
    turn = jax.random.randint(jax.random.fold_in(own, 2), (rows, 1), 0, top)
    return jnp.take_along_axis(table, (jnp.arange(top)[None, :] + turn) % top, axis=1)


def shares(number_of, total, limit, lean, full):
    loads = [(1 << 20) // math.isqrt(grade ** lean) + 1 for grade in range(1, number_of + 1)]
    largest = limit if full else min(limit, max(-(-total // number_of), total * loads[0] // sum(loads)))
    least = 1 if total - largest >= number_of - 1 else 0
    counts, rest = [largest] + [least] * (number_of - 1), total - largest - least * (number_of - 1)
    while rest > 0:
        free = [i for i in range(1, number_of) if counts[i] < largest] or [i for i in range(1, number_of) if counts[i] < limit]
        pool, budget = sum([loads[i] for i in free]), rest
        for i in free:
            addition = min(limit - counts[i], max(1, budget * loads[i] // pool), rest)
            counts[i] = counts[i] + addition
            rest = rest - addition
    return np.array(counts)


def gaussian(own_key, dims, width, most, pieces=(), held_as=jnp.bfloat16):
    gain = levels(own_key, dims, pieces, -0.22, 0.18) if pieces else 1.0
    result = jax.random.normal(own_key, dims, jnp.float32) * width * gain
    return jnp.minimum(jnp.maximum(result, -most), most).astype(held_as)


def setup_inputs(seed: int = 0) -> dict:
    key_of = jax.random.split(jax.random.key(seed), 13)
    queries = draw_queries(jax.random.fold_in(key_of[12], 71), 0)
    keys = draw_keys(jax.random.fold_in(key_of[12], 71), 0)
    values = gaussian(key_of[2], (SEQ, H * HD), 1.0, 6.0, ((0, 16), (1, 16)))
    segments = draw_segments(jax.random.fold_in(key_of[12], 71), 0)
    residual = gaussian(key_of[4], (SEQ, D), 1.0, 6.0, ((0, 256),))
    out_weight = gaussian(key_of[5], (H * HD, D), (H * HD) ** -0.5, 0.125, ((0, 16),))
    norm_gain = jnp.clip(1.0 + 0.18 * jax.random.normal(key_of[6], (D,), jnp.float32), 0.1, 1.9)
    router = gaussian(key_of[7], (D, EXPERTS), D ** -0.5, 0.125, (), jnp.float32)
    routes_keys = jax.random.split(jax.random.fold_in(key_of[8], 1), SEQ // TOK)
    routes_turns = jax.random.permutation(jax.random.fold_in(key_of[8], 3), SEQ // TOK)
    routes = jax.vmap(lambda own, number: deal_out(jax.random.fold_in(key_of[8], 2), own, number, TOK, EXPERTS, TOPK, CAP, 2))(routes_keys, routes_turns).reshape((SEQ, TOPK))
    gate_weight = gaussian(key_of[9], (N_EP, N_CTX, D, FFQ), D ** -0.5, 0.125, ((0, 16), (1, 16)))
    up_weight = gaussian(key_of[10], (N_EP, N_CTX, D, FFQ), D ** -0.5, 0.125, ((0, 16), (1, 16)))
    down_weight = gaussian(key_of[11], (N_EP, N_CTX, FFQ, D), FF ** -0.5, 0.15625, ((0, 16), (1, 16)))
    return {"queries": queries, "keys": keys, "values": values, "segments": segments, "residual": residual, "out_weight": out_weight, "norm_gain": norm_gain, "router": router, "routes": routes, "gate_weight": gate_weight, "up_weight": up_weight, "down_weight": down_weight}


def attend_head(query_h, key_h, value_h, segments):
    positions = jnp.arange(SEQ)
    block = 512 if SEQ % 512 == 0 else SEQ
    scale = HD ** (-0.5)

    def one_block(start):
        q_block = lax.dynamic_slice_in_dim(query_h, start, block)
        q_pos = start + jnp.arange(block)
        q_seg = lax.dynamic_slice_in_dim(segments, start, block)
        scores = jnp.dot(q_block, key_h.T, preferred_element_type=jnp.float32) * scale
        allowed = (q_seg[:, None] == segments[None, :]) & (positions[None, :] <= q_pos[:, None])
        scores = jnp.where(allowed, scores, jnp.float32(-1e+30))
        best = lax.optimization_barrier(jnp.max(scores, axis=1, keepdims=True))
        expo = jnp.where(allowed, jnp.exp(scores - best), jnp.float32(0.0))
        total = lax.optimization_barrier(jnp.sum(expo, axis=1, keepdims=True))
        probs = expo.astype(jnp.bfloat16)
        summed = jnp.dot(probs, value_h, preferred_element_type=jnp.float32)
        return (summed / total).astype(jnp.bfloat16)
    starts = (jnp.arange(SEQ // block) * block).astype(jnp.int32)
    return lax.map(one_block, starts).reshape(SEQ, HD)

def reference(queries, keys, values, segments, residual, out_weight, norm_gain, router, routes, gate_weight, up_weight, down_weight):
    query_t = jnp.transpose(queries.reshape(SEQ, H, HD), (1, 0, 2))
    key_t = jnp.transpose(keys.reshape(SEQ, H, HD), (1, 0, 2))
    value_t = jnp.transpose(values.reshape(SEQ, H, HD), (1, 0, 2))
    heads = lax.map(lambda item: attend_head(item[0], item[1], item[2], segments), (query_t, key_t, value_t))
    attended = jnp.transpose(heads, (1, 0, 2)).reshape(SEQ, H * HD)
    attn = jnp.dot(attended, out_weight, preferred_element_type=jnp.float32)
    stream = residual.astype(jnp.float32) + attn
    normed = (stream * lax.rsqrt(lax.optimization_barrier(jnp.mean(stream * stream, axis=1, keepdims=True)) + 1e-06) * norm_gain).astype(jnp.bfloat16)
    logits = jnp.dot(normed.astype(jnp.float32), router, precision=lax.Precision.HIGHEST)
    gates = jax.nn.sigmoid(jnp.take_along_axis(logits, routes, axis=1))
    weights = gates / lax.optimization_barrier(jnp.sum(gates, axis=1, keepdims=True))
    blocks = SEQ // TOK
    flat = routes.reshape(blocks, TOK * TOPK)
    onehot = (flat[:, :, None] == jnp.arange(EXPERTS, dtype=jnp.int32)[None, None, :]).astype(jnp.int32)
    before = jnp.cumsum(onehot, axis=1).astype(jnp.int32) - onehot
    rank = lax.optimization_barrier(jnp.sum(before * onehot, axis=2)).astype(jnp.int32)
    block_ids = jnp.broadcast_to(jnp.arange(blocks, dtype=jnp.int32)[:, None], (blocks, TOK * TOPK))
    token_ids = (block_ids * TOK + (jnp.arange(TOK * TOPK, dtype=jnp.int32) // TOPK)[None, :]).astype(jnp.int32)
    token_table = jnp.full((blocks, EXPERTS, CAP), SEQ, dtype=jnp.int32).at[block_ids, flat, rank].set(token_ids)
    weight_table = jnp.zeros((blocks, EXPERTS, CAP), jnp.float32).at[block_ids, flat, rank].set(weights.reshape(blocks, TOK * TOPK))
    normed_pad = jnp.concatenate([normed, jnp.zeros((1, D), jnp.bfloat16)], axis=0)
    gate_all = gate_weight.reshape(EXPERTS, SPLIT, D, FFQ)
    up_all = up_weight.reshape(EXPERTS, SPLIT, D, FFQ)
    down_all = down_weight.reshape(EXPERTS, SPLIT, FFQ, D)

    def one_expert(mixed, expert):
        index_rows = token_table[:, expert, :].reshape(-1)
        scale_rows = weight_table[:, expert, :].reshape(-1)
        rows = normed_pad[index_rows]
        total = jnp.zeros((rows.shape[0], D), jnp.float32)
        for piece in range(SPLIT):
            gate = jnp.dot(rows, gate_all[expert, piece], preferred_element_type=jnp.float32)
            upper = jnp.dot(rows, up_all[expert, piece], preferred_element_type=jnp.float32)
            act = (jax.nn.silu(gate) * upper).astype(jnp.bfloat16)
            part = jnp.dot(act, down_all[expert, piece], preferred_element_type=jnp.float32).astype(jnp.bfloat16)
            total = total + part.astype(jnp.float32)
        expert_out = total.astype(jnp.bfloat16).astype(jnp.float32)
        mixed = mixed.at[index_rows].add(scale_rows[:, None] * expert_out)
        return (mixed, None)
    mixed, _ = lax.scan(one_expert, jnp.zeros((SEQ + 1, D), jnp.float32), jnp.arange(EXPERTS, dtype=jnp.int32))
    return (stream + mixed[:SEQ]).astype(jnp.bfloat16)
```

```python
import functools

import jax
import jax.numpy as jnp
from jax import lax
from jax.experimental import pallas as pl
from jax.experimental.pallas import tpu as pltpu
from jax.sharding import PartitionSpec as P

HD = 128
CAP = 6
MESH = pl.DeviceIdType.MESH
ANY = pl.BlockSpec(memory_space=pl.ANY)
BF16 = jnp.bfloat16
F32 = jnp.float32
LOG2E = 1.4426950408889634


def remote(src, dst, send, recv, ctx, ep):
    return pltpu.make_async_remote_copy(
        src_ref=src,
        dst_ref=dst,
        send_sem=send,
        recv_sem=recv,
        device_id=(ctx, ep),
        device_id_type=MESH,
    )


def greet(peers):
    barrier = pltpu.get_barrier_semaphore()
    for ctx, ep in peers:
        pl.semaphore_signal(barrier, inc=1, device_id=(ctx, ep), device_id_type=MESH)
    pl.semaphore_wait(barrier, len(peers))


def params(collective_id, vmem=32 << 20):
    return pltpu.CompilerParams(
        collective_id=collective_id, has_side_effects=True, vmem_limit_bytes=vmem
    )


def gather_kernel(k_ref, v_ref, k_all, v_all, send, recv, local):
    c, e = lax.axis_index("ctx"), lax.axis_index("ep")
    z, x = c // 2, c % 2
    ox = 1 - x
    up, down, side = ((z + 1) % 8) * 2 + x, ((z + 7) % 8) * 2 + x, z * 2 + ox
    greet([(up, e), (down, e), (side, e)])
    own_k = pltpu.make_async_copy(k_ref, k_all.at[c], local.at[0])
    own_v = pltpu.make_async_copy(v_ref, v_all.at[c], local.at[1])
    own_k.start()
    own_v.start()
    started = []
    slots = iter(range(32))

    def go(src, dst, slot, to):
        copy = remote(src, dst, send.at[slot], recv.at[slot], to, e)
        copy.start()
        started.append(copy)
        return copy

    side_k = go(k_ref, k_all.at[c], next(slots), side)
    up_k, down_k, up_v, down_v = {}, {}, {}, {}
    for t in range(1, 5):
        up_k[t] = (next(slots), next(slots))
        down_k[t] = (next(slots), next(slots))
        up_v[t], down_v[t] = next(slots), next(slots)

    copies = {}
    copies["uv", 1] = go(v_ref, v_all.at[c], up_v[1], up)
    copies["dv", 1] = go(v_ref, v_all.at[c], down_v[1], down)
    copies["uk", 1, 0] = go(k_ref, k_all.at[c], up_k[1][0], up)
    copies["dk", 1, 0] = go(k_ref, k_all.at[c], down_k[1][0], down)
    side_v = [go(v_ref, v_all.at[c], next(slots), side)]
    side_k.wait_recv()
    copies["uk", 1, 1] = go(k_all.at[side], k_all.at[side], up_k[1][1], up)
    copies["dk", 1, 1] = go(k_all.at[side], k_all.at[side], down_k[1][1], down)
    extra = iter(range(26, 33))
    for t in range(1, 5):
        below, above = (z + 8 - t) % 8, (z + t) % 8
        if t <= 3:
            copies["uv", t].wait_recv()
            block = v_all.at[below * 2 + x]
            if t <= 2:
                copies["uv", t + 1] = go(block, block, up_v[t + 1], up)
            side_v.append(go(block, block, next(extra), side))
        copies["dv", t].wait_recv()
        block = v_all.at[above * 2 + x]
        if t <= 3:
            copies["dv", t + 1] = go(block, block, down_v[t + 1], down)
        side_v.append(go(block, block, next(extra), side))
        for h, column in ((0, x), (1, ox)):
            copies["uk", t, h].wait_recv()
            block = k_all.at[below * 2 + column]
            if t <= 3:
                copies["uk", t + 1, h] = go(block, block, up_k[t + 1][h], up)
            if t <= 3:
                copies["dk", t, h].wait_recv()
                block = k_all.at[above * 2 + column]
                if t <= 2:
                    copies["dk", t + 1, h] = go(block, block, down_k[t + 1][h], down)
    for copy in side_v:
        copy.wait_recv()
    for copy in started:
        copy.wait_send()
    own_k.wait()
    own_v.wait()


def gather_kv(keys, values):
    out = jax.ShapeDtypeStruct((16,) + keys.shape, BF16)
    return pl.pallas_call(
        gather_kernel,
        out_shape=(out, out),
        in_specs=[ANY, ANY],
        out_specs=(ANY, ANY),
        scratch_shapes=[
            pltpu.SemaphoreType.DMA((34,)),
            pltpu.SemaphoreType.DMA((34,)),
            pltpu.SemaphoreType.DMA((2,)),
        ],
        compiler_params=params(1),
        name="gather_kv",
    )(keys, values)


def attend_kernel(info, q_ref, k_ref, v_ref, qseg_ref, kseg_ref, o_ref, best, total, acc):
    step = pl.program_id(0)
    c, first = info[0], info[1]
    block = c - step
    scale = (HD**-0.5) * LOG2E

    def update(masked, diagonal):
        s = lax.dot_general(
            q_ref[...], k_ref[0], (((1,), (1,)), ((), ())), preferred_element_type=F32
        )
        s = s * scale
        if masked:
            ok = qseg_ref[...] == kseg_ref[0]
            if diagonal:
                rows = lax.broadcasted_iota(jnp.int32, s.shape, 0)
                cols = lax.broadcasted_iota(jnp.int32, s.shape, 1)
                ok = ok & (cols <= rows)
            s = jnp.where(ok, s, -1e30)
        peak = jnp.max(s, axis=1, keepdims=True)
        if diagonal:
            new = peak
            p = jnp.exp2(s - new)
            total[...] = jnp.sum(p, axis=1, keepdims=True)
            acc[...] = jnp.dot(p.astype(BF16), v_ref[0], preferred_element_type=F32)
        else:
            old = best[...]
            new = jnp.maximum(old, peak)
            p = jnp.exp2(s - new)
            factor = jnp.exp2(old - new)
            total[...] = total[...] * factor + jnp.sum(p, axis=1, keepdims=True)
            acc[...] = acc[...] * factor + jnp.dot(
                p.astype(BF16), v_ref[0], preferred_element_type=F32
            )
        best[...] = new

    @pl.when(step == 0)
    def _():
        update(True, True)

    inside = (step > 0) & (block >= first)
    same = block >= info[2]

    @pl.when(inside & same)
    def _():
        update(False, False)

    @pl.when(inside & jnp.logical_not(same))
    def _():
        update(True, False)

    @pl.when(step == pl.num_programs(0) - 1)
    def _():
        o_ref[...] = (acc[...] / total[...]).astype(BF16)


def attend(queries, k_all, v_all, segments):
    rows = queries.shape[0]
    c = lax.axis_index("ctx")
    start = c * rows
    q_seg = lax.dynamic_slice_in_dim(segments, start, rows)
    first = jnp.sum((segments < q_seg[0]).astype(jnp.int32)) // rows
    same = (jnp.sum((segments < q_seg[rows - 1]).astype(jnp.int32)) + rows - 1) // rows
    info = jnp.stack([c, first, same]).astype(jnp.int32)

    def kv(i, info):
        return (jnp.maximum(info[0] - i, info[1]), 0, 0)

    return pl.pallas_call(
        attend_kernel,
        out_shape=jax.ShapeDtypeStruct(queries.shape, BF16),
        grid_spec=pltpu.PrefetchScalarGridSpec(
            num_scalar_prefetch=1,
            grid=(16,),
            in_specs=[
                pl.BlockSpec((rows, HD), lambda i, info: (0, 0)),
                pl.BlockSpec((1, rows, HD), kv),
                pl.BlockSpec((1, rows, HD), kv),
                pl.BlockSpec((rows, 1), lambda i, info: (0, 0)),
                pl.BlockSpec((1, 1, rows), kv),
            ],
            out_specs=pl.BlockSpec((rows, HD), lambda i, info: (0, 0)),
            scratch_shapes=[
                pltpu.VMEM((rows, 1), F32),
                pltpu.VMEM((rows, 1), F32),
                pltpu.VMEM((rows, HD), F32),
            ],
        ),
        compiler_params=pltpu.CompilerParams(vmem_limit_bytes=32 << 20),
        name="attend",
    )(info, queries, k_all, v_all, q_seg.reshape(rows, 1), segments.reshape(16, 1, rows))


def heads_kernel(a_ref, r_ref, a_out, r_out, send, recv, rsend, rrecv, local):
    c, e = lax.axis_index("ctx"), lax.axis_index("ep")
    core, m = e % 2, e // 2
    greet([(c, (e + d) % 16) for d in range(1, 16)])
    own_a = pltpu.make_async_copy(a_ref.at[e], a_out.at[e], local.at[0])
    own_r = pltpu.make_async_copy(r_ref, r_out.at[m], local.at[1])
    own_a.start()
    own_r.start()
    copies = []
    for d in range(1, 16):
        to = (e + d) % 16
        copies.append(remote(a_ref.at[to], a_out.at[e], send.at[d], recv.at[d], c, to))
        copies[-1].start()
    for d in range(1, 8):
        to = ((m + d) % 8) * 2 + core
        copies.append(remote(r_ref, r_out.at[m], rsend.at[d], rrecv.at[d], c, to))
        copies[-1].start()
    for copy in copies:
        copy.wait()
    own_a.wait()
    own_r.wait()


def exchange_heads(attended, routes):
    return pl.pallas_call(
        heads_kernel,
        out_shape=(
            jax.ShapeDtypeStruct(attended.shape, BF16),
            jax.ShapeDtypeStruct((8,) + routes.shape, jnp.int32),
        ),
        in_specs=[ANY, ANY],
        out_specs=(ANY, ANY),
        scratch_shapes=[
            pltpu.SemaphoreType.DMA((16,)),
            pltpu.SemaphoreType.DMA((16,)),
            pltpu.SemaphoreType.DMA((8,)),
            pltpu.SemaphoreType.DMA((8,)),
            pltpu.SemaphoreType.DMA((2,)),
        ],
        compiler_params=params(2),
        name="exchange_heads",
    )(attended, routes)


def group_kernel(scatter, a_ref, a_out, send, recv, local):
    c, e = lax.axis_index("ctx"), lax.axis_index("ep")
    core, m = e % 2, e // 2
    greet([(c, ((m + d) % 8) * 2 + core) for d in range(1, 8)])
    own = pltpu.make_async_copy(a_ref.at[m] if scatter else a_ref, a_out.at[m], local)
    own.start()
    copies = []
    for d in range(1, 8):
        to = (m + d) % 8
        src = a_ref.at[to] if scatter else a_ref
        copies.append(remote(src, a_out.at[m], send.at[d], recv.at[d], c, to * 2 + core))
        copies[-1].start()
    for copy in copies:
        copy.wait()
    own.wait()


def group_exchange(rows, scatter, collective_id):
    shape = rows.shape[-2:]
    return pl.pallas_call(
        functools.partial(group_kernel, scatter),
        out_shape=jax.ShapeDtypeStruct((8,) + shape, rows.dtype),
        in_specs=[ANY],
        out_specs=ANY,
        scratch_shapes=[
            pltpu.SemaphoreType.DMA((8,)),
            pltpu.SemaphoreType.DMA((8,)),
            pltpu.SemaphoreType.DMA,
        ],
        compiler_params=params(collective_id),
        name="group_scatter" if scatter else "group_gather",
    )(rows)


def project_kernel(a_ref, w_ref, res_ref, gain_ref, stream_ref, normed_ref, acc):
    step = pl.program_id(0)

    @pl.when(step == 0)
    def _():
        acc[...] = res_ref[...].astype(F32)

    part = jnp.dot(a_ref[0], w_ref[0:HD, :], preferred_element_type=F32)
    for h in range(1, a_ref.shape[0]):
        part += jnp.dot(
            a_ref[h], w_ref[h * HD : (h + 1) * HD, :], preferred_element_type=F32
        )
    acc[...] += part

    @pl.when(step == pl.num_programs(0) - 1)
    def _():
        s = acc[...]
        stream_ref[...] = s
        mean = jnp.mean(s * s, axis=1, keepdims=True)
        normed_ref[...] = (s * lax.rsqrt(mean + 1e-06) * gain_ref[...]).astype(BF16)


def project(heads, weight, residual, gain):
    tok, width = residual.shape
    n = heads.shape[0]
    per = 2
    return pl.pallas_call(
        project_kernel,
        out_shape=(
            jax.ShapeDtypeStruct((tok, width), F32),
            jax.ShapeDtypeStruct((tok, width), BF16),
        ),
        grid=(n // per,),
        in_specs=[
            pl.BlockSpec((per, tok, HD), lambda i: (i, 0, 0)),
            pl.BlockSpec((per * HD, width), lambda i: (i, 0)),
            pl.BlockSpec((tok, width), lambda i: (0, 0)),
            pl.BlockSpec((1, width), lambda i: (0, 0)),
        ],
        out_specs=(
            pl.BlockSpec((tok, width), lambda i: (0, 0)),
            pl.BlockSpec((tok, width), lambda i: (0, 0)),
        ),
        scratch_shapes=[pltpu.VMEM((tok, width), F32)],
        compiler_params=pltpu.CompilerParams(vmem_limit_bytes=32 << 20),
        name="project",
    )(heads, weight, residual, gain.reshape(1, width))


def dispatch_kernel(tok_ref, route_ref, router_ref, column_ref, rows_ref, weight_ref):
    count = tok_ref.shape[0]
    experts = router_ref.shape[1]
    width = column_ref.shape[1]
    routes = route_ref[...]
    ids = lax.broadcasted_iota(jnp.int32, (count, experts), 1)
    named = routes[:, 0:1] == ids
    for k in range(1, 6):
        named = named | (routes[:, k : k + 1] == ids)
    named = named.astype(F32)
    t0 = lax.broadcasted_iota(jnp.int32, (count, count), 0)
    t1 = lax.broadcasted_iota(jnp.int32, (count, count), 1)
    before = ((t1 < t0) & (t1 // 32 == t0 // 32)).astype(BF16)
    rank = jnp.dot(before, named.astype(BF16), preferred_element_type=F32)
    owner = lax.broadcasted_iota(jnp.int32, (count, experts), 0) // 32
    place = jnp.where(named > 0, rank + (owner * CAP).astype(F32), -1.0)
    expert_of = column_ref[0:1, :]
    slot_of = column_ref[1:2, :].astype(F32)
    pick = (
        lax.broadcasted_iota(jnp.int32, (experts, width), 0) == expert_of
    ).astype(BF16)
    spread = jnp.dot(place.astype(BF16), pick, preferred_element_type=F32)
    chosen = spread == slot_of
    rows_ref[...] = lax.dot_general(
        chosen.astype(BF16),
        tok_ref[...],
        (((0,), (0,)), ((), ())),
        preferred_element_type=F32,
    ).astype(BF16)
    router = router_ref[...]
    high = router.astype(BF16)
    low = (router - high.astype(F32)).astype(BF16)
    tokens = tok_ref[...]
    logits = jnp.dot(tokens, high, preferred_element_type=F32) + jnp.dot(
        tokens, low, preferred_element_type=F32
    )
    gates = named * jax.nn.sigmoid(logits)
    weights = gates / jnp.sum(gates, axis=1, keepdims=True)
    high = weights.astype(BF16)
    low = (weights - high.astype(F32)).astype(BF16)
    spread = jnp.dot(high, pick, preferred_element_type=F32) + jnp.dot(
        low, pick, preferred_element_type=F32
    )
    weight_ref[...] = jnp.where(chosen, spread, 0.0)


def dispatch(tokens, routes, router, columns):
    count, width = tokens.shape
    n = columns.shape[1]
    return pl.pallas_call(
        dispatch_kernel,
        out_shape=(
            jax.ShapeDtypeStruct((n, width), BF16),
            jax.ShapeDtypeStruct((count, n), F32),
        ),
        compiler_params=pltpu.CompilerParams(vmem_limit_bytes=32 << 20),
        name="dispatch",
    )(tokens, routes, router, columns)


def combine_kernel(weight_ref, rows_ref, out_ref):
    weights = weight_ref[...]
    high = weights.astype(BF16)
    low = (weights - high.astype(F32)).astype(BF16)
    rows = rows_ref[...]
    out_ref[...] = (
        jnp.dot(high, rows, preferred_element_type=F32)
        + jnp.dot(low, rows, preferred_element_type=F32)
    ).astype(BF16)


def combine(weights, rows):
    return pl.pallas_call(
        combine_kernel,
        out_shape=jax.ShapeDtypeStruct((weights.shape[0], rows.shape[1]), BF16),
        compiler_params=pltpu.CompilerParams(vmem_limit_bytes=32 << 20),
        name="combine",
    )(weights, rows)


def final_kernel(stream_ref, part_ref, out_ref):
    total = stream_ref[...]
    for m in range(8):
        total = total + part_ref[m].astype(F32)
    out_ref[...] = total.astype(BF16)


def finish(stream, parts):
    return pl.pallas_call(
        final_kernel,
        out_shape=jax.ShapeDtypeStruct(stream.shape, BF16),
        compiler_params=pltpu.CompilerParams(vmem_limit_bytes=32 << 20),
        name="finish",
    )(stream, parts)


def away(i):
    half = (i + 1) // 2
    return half * (2 * (i % 2) - 1)


def expert_kernel(
    rows_ref,
    wg_ref,
    wu_ref,
    wd_ref,
    back_ref,
    xs,
    ps,
    from_core,
    from_side,
    sums,
    done,
    wg,
    wu,
    wd,
    z_send,
    z_recv,
    x_send,
    x_recv,
    s_send,
    s_recv,
    c_send,
    c_recv,
    f_send,
    f_recv,
    b_send,
    b_recv,
    local,
):
    c, e = lax.axis_index("ctx"), lax.axis_index("ep")
    z, x = c // 2, c % 2
    side, other = z * 2 + (1 - x), e + 1 - 2 * (e % 2)
    n = 8
    loads = [
        pltpu.make_async_copy(wg_ref, wg, local.at[0]),
        pltpu.make_async_copy(wu_ref, wu, local.at[1]),
        pltpu.make_async_copy(wd_ref, wd, local.at[2]),
    ]
    for load in loads:
        load.start()
    own = pltpu.make_async_copy(rows_ref.at[0], xs.at[0, 0], local.at[3])
    own.start()
    peers = [(((z + d) % n) * 2 + x, e) for d in range(1, n)]
    greet(peers + [(side, e), (c, other)])

    def out(i):
        to = ((z + n - away(i)) % n) * 2 + x
        return remote(rows_ref.at[i], xs.at[i, 0], z_send.at[i], z_recv.at[i], to, e)

    def to_side(i):
        return remote(xs.at[i, 0], xs.at[i, 1], x_send.at[i], x_recv.at[i], side, e)

    def to_core(i, q):
        return remote(
            xs.at[i, q], xs.at[i, q + 2], s_send.at[i, q], s_recv.at[i, q], c, other
        )

    def sum_core(i):
        return remote(
            ps.at[i, pl.ds(2, 2)], from_core.at[i], c_send.at[i], c_recv.at[i], c, other
        )

    def sum_side(i):
        return remote(
            sums.at[i], from_side.at[i], f_send.at[i], f_recv.at[i], side, e
        )

    def home(i):
        to = ((z + n + away(i)) % n) * 2 + x
        return remote(done.at[i], back_ref.at[i], b_send.at[i], b_recv.at[i], to, e)

    for i in range(1, n):
        out(i).start()
    own.wait()
    for load in loads:
        load.wait()

    def step(s, carry):
        @pl.when(s < n)
        def _():
            @pl.when(s > 0)
            def _():
                out(s).wait_recv()

            to_side(s).start()
            to_core(s, 0).start()

        @pl.when((s >= 1) & (s < n + 1))
        def _():
            i = s - 1
            to_side(i).wait_recv()
            to_core(i, 1).start()

        @pl.when((s >= 2) & (s < n + 2))
        def _():
            i = s - 2
            to_core(i, 0).wait_recv()
            to_core(i, 1).wait_recv()
            shape = xs.shape[1:]
            rows = xs[i].reshape(shape[0] * shape[1], shape[2])
            gate = jnp.dot(rows, wg[...], preferred_element_type=F32)
            upper = jnp.dot(rows, wu[...], preferred_element_type=F32)
            act = (gate / (1.0 + jnp.exp(-gate)) * upper).astype(BF16)
            part = jnp.dot(act, wd[...], preferred_element_type=F32)
            ps[i] = part.astype(BF16).reshape(shape)
            sum_core(i).start()

        @pl.when((s >= 3) & (s < n + 3))
        def _():
            i = s - 3
            sum_core(i).wait_recv()
            sums[i] = (ps[i, 1].astype(F32) + from_core[i, 1].astype(F32)).astype(BF16)
            sum_side(i).start()

        @pl.when(s >= 4)
        def _():
            i = s - 4
            sum_side(i).wait_recv()
            done[i] = (
                ps[i, 0].astype(F32) + from_core[i, 0].astype(F32) + from_side[i].astype(F32)
            ).astype(BF16)

            @pl.when(i > 0)
            def _():
                home(i).start()

        return carry

    lax.fori_loop(0, n + 4, step, 0)
    last = pltpu.make_async_copy(done.at[0], back_ref.at[0], local.at[3])
    last.start()

    def drain(i, carry):
        to_side(i).wait_send()
        to_core(i, 0).wait_send()
        to_core(i, 1).wait_send()
        sum_core(i).wait_send()
        sum_side(i).wait_send()

        @pl.when(i > 0)
        def _():
            out(i).wait_send()
            home(i).wait()

        return carry

    lax.fori_loop(0, n, drain, 0)
    last.wait()


def experts(rows, wg, wu, wd):
    n, cap, width = rows.shape
    dma = pltpu.SemaphoreType.DMA
    return pl.pallas_call(
        expert_kernel,
        out_shape=jax.ShapeDtypeStruct(rows.shape, BF16),
        in_specs=[ANY] * 4,
        out_specs=ANY,
        scratch_shapes=[
            pltpu.VMEM((n, 4, cap, width), BF16),
            pltpu.VMEM((n, 4, cap, width), BF16),
            pltpu.VMEM((n, 2, cap, width), BF16),
            pltpu.VMEM((n, cap, width), BF16),
            pltpu.VMEM((n, cap, width), BF16),
            pltpu.VMEM((n, cap, width), BF16),
            pltpu.VMEM(wg.shape, BF16),
            pltpu.VMEM(wu.shape, BF16),
            pltpu.VMEM(wd.shape, BF16),
            dma((n,)),
            dma((n,)),
            dma((n,)),
            dma((n,)),
            dma((n, 2)),
            dma((n, 2)),
            dma((n,)),
            dma((n,)),
            dma((n,)),
            dma((n,)),
            dma((n,)),
            dma((n,)),
            dma((4,)),
        ],
        compiler_params=params(3, 56 << 20),
        name="experts",
    )(rows, wg, wu, wd)


def swap_pairs():
    pairs = []
    for c in range(16):
        for e in range(16):
            move = ((c >> 1) & 1) != (e & 1)
            to = ((c ^ 2) * 16 + (e ^ 1)) if move else c * 16 + e
            pairs.append((c * 16 + e, to))
    return pairs


def body(
    queries,
    keys,
    values,
    segments,
    residual,
    out_weight,
    norm_gain,
    router,
    routes,
    gate_weight,
    up_weight,
    down_weight,
):
    tok, width = residual.shape
    c, e = lax.axis_index("ctx"), lax.axis_index("ep")
    pairs = swap_pairs()
    wg = lax.ppermute(gate_weight[0, 0], ("ctx", "ep"), pairs)
    wu = lax.ppermute(up_weight[0, 0], ("ctx", "ep"), pairs)
    wd = lax.ppermute(down_weight[0, 0], ("ctx", "ep"), pairs)
    weight = lax.all_gather(out_weight, "ep", axis=0, tiled=True)
    k_all, v_all = gather_kv(keys, values)
    attended = attend(queries, k_all, v_all, segments)
    padded = jnp.pad(routes, ((0, 0), (0, 128 - routes.shape[1])), constant_values=-1)
    heads, group_routes = exchange_heads(attended.reshape(16, tok, HD), padded)
    stream, normed = project(heads, weight, residual, norm_gain)
    tokens = group_exchange(normed, False, 4).reshape(8 * tok, width)
    block = jnp.arange(8, dtype=jnp.int32)
    at = (c // 2 + 8 - away(block)) % 8
    expert = 8 * (e // 2) + 4 * (at % 2) + at // 2
    slots = 8 * CAP
    columns = jnp.stack(
        [
            jnp.repeat(expert, slots),
            jnp.tile(jnp.arange(slots, dtype=jnp.int32), 8),
        ]
    ).astype(jnp.int32)
    rows, weights = dispatch(tokens, group_routes.reshape(8 * tok, 128), router, columns)
    back = experts(rows.reshape(8, slots, width), wg, wu, wd)
    mixed = combine(weights, back.reshape(8 * slots, width))
    parts = group_exchange(mixed.reshape(8, tok, width), True, 5)
    return finish(stream, parts)


def solution(mesh):
    placed = (
        P("ctx", "ep"),
        P("ctx", "ep"),
        P("ctx", "ep"),
        P(),
        P(("ctx", "ep"), None),
        P("ep", None),
        P(),
        P(),
        P(("ctx", "ep"), None),
        P("ep", "ctx", None, None),
        P("ep", "ctx", None, None),
        P("ep", "ctx", None, None),
    )
    return jax.shard_map(
        body, mesh=mesh, in_specs=placed, out_specs=P(("ctx", "ep"), None), check_vma=False
    )
```

```python
import jax
import jax.numpy as jnp
from jax import lax
from jax.experimental import pallas as pl
from jax.experimental.pallas import tpu as pltpu
from jax.sharding import PartitionSpec as P

HD = 128
CAP = 6
WINDOW = 2
MESH = pl.DeviceIdType.MESH
ANY = pl.BlockSpec(memory_space=pl.ANY)
BF16 = jnp.bfloat16
F32 = jnp.float32
LOG2E = 1.4426950408889634


def remote(src, dst, send, recv, ctx, ep):
    return pltpu.make_async_remote_copy(
        src_ref=src,
        dst_ref=dst,
        send_sem=send,
        recv_sem=recv,
        device_id=(ctx, ep),
        device_id_type=MESH,
    )


def greet(peers):
    barrier = pltpu.get_barrier_semaphore()
    for ctx, ep in peers:
        pl.semaphore_signal(barrier, inc=1, device_id=(ctx, ep), device_id_type=MESH)
    pl.semaphore_wait(barrier, len(peers))


def params(collective_id, vmem=60 << 20):
    return pltpu.CompilerParams(
        collective_id=collective_id, has_side_effects=True, vmem_limit_bytes=vmem
    )


def device(c, e, dz=0, dy=0, mirror=False):
    z, x, y, x_hi, core = c // 2, c % 2, e // 4, (e // 2) % 2, e % 2
    if mirror:
        x, x_hi = 1 - x, 1 - x_hi
    return ((z + dz + 8) % 8) * 2 + x, ((y + dy + 4) % 4) * 4 + x_hi * 2 + core


GROUP = [(dy, side) for dy in range(4) for side in (False, True)][1:]


def slot_of(dy, side):
    return ((dy + 4) % 4) * 2 + int(side)


def front_kernel(
    q_ref,
    k_ref,
    v_ref,
    seg_ref,
    w_ref,
    res_ref,
    gain_ref,
    route_ref,
    router_ref,
    own_wg,
    own_wu,
    stream_ref,
    rows_ref,
    weight_ref,
    moved_wg,
    moved_wu,
    kv,
    queries,
    away_acc,
    away_stat,
    there_acc,
    there_stat,
    w,
    att,
    heads,
    normed,
    tok_ref,
    routes_ref,
    best,
    total,
    acc,
    kv_send,
    kv_recv,
    w_send,
    w_recv,
    h_send,
    h_recv,
    r_send,
    r_recv,
    t_send,
    t_recv,
    m_send,
    m_recv,
):
    c, e = lax.axis_index("ctx"), lax.axis_index("ep")
    z, x = c // 2, c % 2
    ox = 1 - x
    tok = res_ref.shape[0]
    rows = q_ref.shape[0]
    per = rows // 128
    scale = (HD**-0.5) * LOG2E
    up, down, side = (((z + 1) % 8) * 2 + x, e), (((z + 7) % 8) * 2 + x, e), (z * 2 + ox, e)
    north, south = device(c, e, dy=1), device(c, e, dy=-1)
    across = device(c, e, mirror=True)
    sibling = (c, e + 1 - 2 * (e % 2))
    diagonal = (c + 2 - 4 * (z % 2), e + 1 - 2 * (e % 2))
    everyone = [(c, (e + d) % 16) for d in range(1, 16)]
    everyone += [device(c, e, dy=dy, mirror=True) for dy in range(4)]
    greet(everyone + [up, down, side, diagonal])
    started = []

    def line(send, recv):
        count = [0]

        def go(src, dst, to):
            i = count[0]
            count[0] += 1
            copy = remote(src, dst, send.at[i], recv.at[i], *to)
            copy.start()
            started.append(copy)
            return copy

        return go

    go = line(kv_send, kv_recv)
    go_w = line(w_send, w_recv)
    go_r = line(r_send, r_recv)
    go_t = line(t_send, t_recv)

    kv[z, 0] = k_ref[...]
    kv[z, 1] = v_ref[...]
    ask = go(q_ref, queries.at[1], side)
    ups = {1: go(kv.at[z], kv.at[z], up)}
    downs = {1: go(kv.at[z], kv.at[z], down)}
    queries[0] = q_ref[...]

    w[e] = w_ref[...]
    half = w_ref.shape[0] // 2
    own_up = go_w(w.at[e], w.at[e], north)
    own_down = go_w(w.at[e], w.at[e], south)
    crossing = go_w(w.at[e], w.at[e], across)
    shared = [go_w(w.at[e], w.at[e], sibling)]
    e_across = across[1]

    def at_y(base, dy):
        return ((base // 4 + dy + 4) % 4) * 4 + base % 4

    routes = [
        go_r(route_ref, routes_ref.at[slot_of(-dy, far)], device(c, e, dy=dy, mirror=far))
        for dy, far in GROUP
    ]
    routes_ref[0] = route_ref[...]

    moved = (z % 2) != (e % 2)
    swap = [
        remote(src, dst, m_send.at[i], m_recv.at[i], *diagonal)
        for i, (src, dst) in enumerate(
            ((own_wg, moved_wg), (own_wu, moved_wu))
        )
    ]

    def seg_row(block):
        parts = [seg_ref[pl.ds(block * per + i, 1), :] for i in range(per)]
        return jnp.concatenate(parts, axis=1)

    def column(row):
        return jnp.broadcast_to(row, (8, rows)).T[:, 0:1]

    q_seg = jnp.concatenate([column(seg_row(c)), column(seg_row(side[0]))], axis=0)

    def scores(plane):
        s = lax.dot_general(
            queries[...].reshape(2 * rows, HD),
            kv[plane, 0],
            (((1,), (1,)), ((), ())),
            preferred_element_type=F32,
        )
        return s * scale, q_seg == seg_row(plane * 2 + x)

    def tile(plane, wanted):
        @pl.when(wanted)
        def _():
            s, same = scores(plane)
            s = jnp.where(same, s, -1e30)
            old = best[...]
            new = jnp.maximum(old, jnp.max(s, axis=1, keepdims=True))
            p = jnp.exp2(s - new)
            factor = jnp.exp2(old - new)
            best[...] = new
            total[...] = total[...] * factor + jnp.sum(p, axis=1, keepdims=True)
            acc[...] = acc[...] * factor + jnp.dot(
                p.astype(BF16), kv[plane, 1], preferred_element_type=F32
            )

    ask.wait_recv()
    s, same = scores(z)
    i0 = lax.broadcasted_iota(jnp.int32, s.shape, 0)
    i1 = lax.broadcasted_iota(jnp.int32, s.shape, 1)
    reach = jnp.where(i0 < rows, i0, jnp.where(x == 0, rows, -1))
    s = jnp.where(same & (i1 <= reach), s, -1e30)
    new = jnp.maximum(jnp.max(s, axis=1, keepdims=True), -1e29)
    p = jnp.exp2(s - new)
    best[...] = new
    total[...] = jnp.sum(p, axis=1, keepdims=True)
    acc[...] = jnp.dot(p.astype(BF16), kv[z, 1], preferred_element_type=F32)

    for t in range(1, 5):
        below, above = (z + 8 - t) % 8, (z + t) % 8
        ups[t].wait_recv()
        if t <= 2:
            ups[t + 1] = go(kv.at[below], kv.at[below], up)
        elif t == 3:
            ups[4] = go(kv.at[below, 0], kv.at[below, 0], up)
        downs[t].wait_recv()
        if t <= 2:
            downs[t + 1] = go(kv.at[above], kv.at[above], down)
        elif t == 3:
            downs[4] = go(kv.at[above, 1], kv.at[above, 1], down)

            @pl.when(moved)
            def _():
                for copy in swap:
                    copy.start()

        if t == 2:
            crossing.wait_recv()
            far_up = go_w(w.at[e_across], w.at[e_across], north)
            far_down = go_w(w.at[e_across], w.at[e_across], south)
            shared.append(go_w(w.at[e_across], w.at[e_across], sibling))
        tile(below, z >= t)
        if t <= 3:
            tile(above, z + t >= 8)
        if t == 2 or t == 4:
            base = e if t == 2 else e_across
            (own_up if t == 2 else far_up).wait_recv()
            here = w.at[at_y(base, -1), pl.ds(0, half)]
            second_up = go_w(here, here, north)
            here = w.at[at_y(base, -1)]
            shared.append(go_w(here, here, sibling))
            (own_down if t == 2 else far_down).wait_recv()
            here = w.at[at_y(base, 1), pl.ds(half, half)]
            second_down = go_w(here, here, south)
            here = w.at[at_y(base, 1)]
            shared.append(go_w(here, here, sibling))
            if t == 2:
                seconds = [(second_up, second_down, e)]
            else:
                seconds.append((second_up, second_down, e_across))
        if t == 4:
            away_acc[...] = acc[rows : 2 * rows, :].astype(BF16)
            lane = lax.broadcasted_iota(jnp.int32, (rows, HD), 1)
            stat = jnp.where(
                lane == 0, best[rows : 2 * rows, :], total[rows : 2 * rows, :]
            )
            away_stat[...] = stat.T[0:8, :]
            give_acc = go(away_acc, there_acc, side)
            give_stat = go(away_stat, there_stat, side)
    give_acc.wait_recv()
    give_stat.wait_recv()
    stat = there_stat[...].T
    b0, b1 = best[0:rows, :], stat[:, 0:1]
    new = jnp.maximum(b0, b1)
    f0, f1 = jnp.exp2(b0 - new), jnp.exp2(b1 - new)
    whole = total[0:rows, :] * f0 + stat[:, 1:2] * f1
    att[...] = (
        (acc[0:rows, :] * f0 + there_acc[...].astype(F32) * f1) / whole
    ).astype(BF16)

    def mine(of):
        return pl.ds(pl.multiple_of(of * tok, tok), tok)

    arrivals = []
    for d in range(1, 16):
        to = (e + d) % 16
        copy = remote(att.at[mine(to)], heads.at[e], h_send.at[d], h_recv.at[d], c, to)
        copy.start()
        started.append(copy)
        arrivals.append(copy)
    heads[e] = att[mine(e), :]
    for second_up, second_down, base in seconds:
        second_up.wait_recv()
        second_down.wait_recv()
        here = w.at[at_y(base, 2)]
        shared.append(go_w(here, here, sibling))
    for copy in arrivals:
        copy.wait_recv()
    for copy in shared:
        copy.wait_recv()

    def add_head(h, carry):
        return carry + jnp.dot(heads[h], w[h], preferred_element_type=F32)

    s = lax.fori_loop(0, 16, add_head, res_ref[...].astype(F32))
    stream_ref[...] = s
    mean = jnp.mean(s * s, axis=1, keepdims=True)
    normed[...] = (s * lax.rsqrt(mean + 1e-06) * gain_ref[...]).astype(BF16)

    lower, upper = pl.ds(0, tok // 2), pl.ds(tok // 2, tok // 2)
    crossing = go_t(normed, tok_ref.at[1], across)
    arrive_up = [go_t(normed, tok_ref.at[slot_of(-1, 0)], north)]
    arrive_down = [go_t(normed, tok_ref.at[slot_of(1, 0)], south)]
    tok_ref[0] = normed[...]
    crossing.wait_recv()
    arrive_up.append(go_t(tok_ref.at[1], tok_ref.at[slot_of(-1, 1)], north))
    arrive_down.append(go_t(tok_ref.at[1], tok_ref.at[slot_of(1, 1)], south))
    last = []
    for far in (0, 1):
        arrive_up[far].wait_recv()
        here, there = tok_ref.at[slot_of(-1, far)], tok_ref.at[slot_of(2, far)]
        last.append(go_t(here.at[lower], there.at[lower], north))
        arrive_down[far].wait_recv()
        here = tok_ref.at[slot_of(1, far)]
        last.append(go_t(here.at[upper], there.at[upper], south))
    for copy in last + routes:
        copy.wait_recv()
    tokens = tok_ref[...].reshape(8 * tok, tok_ref.shape[2])
    chosen, weights = placement(
        z,
        8 * (e // 2),
        routes_ref[...].reshape(8 * tok, 128),
        router_ref.shape[0],
        tokens,
        router_ref[...],
    )
    rows_ref[...] = lax.dot_general(
        jnp.where(chosen, 1.0, 0.0).astype(BF16),
        tokens,
        (((0,), (0,)), ((), ())),
        preferred_element_type=F32,
    ).astype(BF16)
    weight_ref[...] = weights
    for copy in started:
        copy.wait_send()

    @pl.when(moved)
    def _():
        for copy in swap:
            copy.wait()


def front(
    queries, keys, values, segments, out_weight, residual, gain, routes, router, own
):
    rows = queries.shape[0]
    tok, width = residual.shape
    slots = 64 * CAP
    vmem = pl.BlockSpec(memory_space=pltpu.VMEM)
    dma = pltpu.SemaphoreType.DMA
    return pl.pallas_call(
        front_kernel,
        out_shape=(
            jax.ShapeDtypeStruct((tok, width), F32),
            jax.ShapeDtypeStruct((slots, width), BF16),
            jax.ShapeDtypeStruct((8 * tok, slots), F32),
            *[jax.ShapeDtypeStruct(w.shape, w.dtype) for w in own],
        ),
        in_specs=[vmem] * 9 + [ANY] * 2,
        out_specs=(vmem, vmem, vmem, ANY, ANY),
        scratch_shapes=[
            pltpu.VMEM((8, 2, rows, HD), BF16),
            pltpu.VMEM((2, rows, HD), BF16),
            pltpu.VMEM((rows, HD), BF16),
            pltpu.VMEM((8, rows), F32),
            pltpu.VMEM((rows, HD), BF16),
            pltpu.VMEM((8, rows), F32),
            pltpu.VMEM((16,) + out_weight.shape, BF16),
            pltpu.VMEM((rows, HD), BF16),
            pltpu.VMEM((16, tok, HD), BF16),
            pltpu.VMEM((tok, width), BF16),
            pltpu.VMEM((8, tok, width), BF16),
            pltpu.VMEM((8,) + routes.shape, jnp.int32),
            pltpu.VMEM((2 * rows, 1), F32),
            pltpu.VMEM((2 * rows, 1), F32),
            pltpu.VMEM((2 * rows, HD), F32),
            dma((11,)),
            dma((11,)),
            dma((18,)),
            dma((18,)),
            dma((16,)),
            dma((16,)),
            dma((7,)),
            dma((7,)),
            dma((9,)),
            dma((9,)),
            dma((2,)),
            dma((2,)),
        ],
        compiler_params=params(1),
        name="front",
    )(
        queries,
        keys,
        values,
        segments.reshape(-1, 128),
        out_weight,
        residual,
        gain.reshape(1, width),
        routes,
        router,
        *own,
    )


def placement(z, first, routes, experts, tokens, router):
    count = routes.shape[0]
    slots = 8 * CAP
    width = 8 * slots
    ids = lax.broadcasted_iota(jnp.int32, (count, experts), 1)
    named = routes[:, 0:1] == ids
    for k in range(1, 6):
        named = named | (routes[:, k : k + 1] == ids)
    named = jnp.where(named, 1.0, 0.0)
    t0 = lax.broadcasted_iota(jnp.int32, (count, count), 0)
    t1 = lax.broadcasted_iota(jnp.int32, (count, count), 1)
    before = jnp.where((t1 < t0) & ((t1 >> 5) == (t0 >> 5)), 1.0, 0.0).astype(BF16)
    rank = jnp.dot(before, named.astype(BF16), preferred_element_type=F32)
    owner = lax.broadcasted_iota(jnp.int32, (count, experts), 0) >> 5
    place = jnp.where(named > 0, rank + (owner * CAP).astype(F32), -1.0)
    col = lax.broadcasted_iota(jnp.int32, (experts, width), 1)
    block = jnp.zeros_like(col)
    for k in range(1, 8):
        block = block + jnp.where(col >= k * slots, 1, 0)
    at = (z + 8 - ((block + 1) >> 1) * (2 * (block & 1) - 1)) & 7
    expert = first + 4 * (at & 1) + (at >> 1)
    pick = jnp.where(
        lax.broadcasted_iota(jnp.int32, (experts, width), 0) == expert, 1.0, 0.0
    ).astype(BF16)
    spread = jnp.dot(place.astype(BF16), pick, preferred_element_type=F32)
    chosen = spread == (col[0:1, :] - slots * block[0:1, :]).astype(F32)
    high = router.astype(BF16)
    low = (router - high.astype(F32)).astype(BF16)
    dims = (((1,), (1,)), ((), ()))
    logits = lax.dot_general(
        tokens, high, dims, preferred_element_type=F32
    ) + lax.dot_general(tokens, low, dims, preferred_element_type=F32)
    gates = named * jax.nn.sigmoid(logits)
    weights = gates / jnp.sum(gates, axis=1, keepdims=True)
    high = weights.astype(BF16)
    low = (weights - high.astype(F32)).astype(BF16)
    spread = jnp.dot(high, pick, preferred_element_type=F32) + jnp.dot(
        low, pick, preferred_element_type=F32
    )
    return chosen, jnp.where(chosen, spread, 0.0)


def combine_kernel(weight_ref, rows_ref, out_ref):
    weights = weight_ref[...]
    high = weights.astype(BF16)
    low = (weights - high.astype(F32)).astype(BF16)
    rows = rows_ref[...]
    out_ref[...] = (
        jnp.dot(high, rows, preferred_element_type=F32)
        + jnp.dot(low, rows, preferred_element_type=F32)
    ).astype(BF16)


def combine(weights, rows):
    return pl.pallas_call(
        combine_kernel,
        out_shape=jax.ShapeDtypeStruct((weights.shape[0], rows.shape[1]), BF16),
        compiler_params=pltpu.CompilerParams(vmem_limit_bytes=32 << 20),
        name="combine",
    )(weights, rows)


def final_kernel(stream_ref, part_ref, out_ref):
    total = stream_ref[...]
    for m in range(8):
        total = total + part_ref[m].astype(F32)
    out_ref[...] = total.astype(BF16)


def finish(stream, parts):
    return pl.pallas_call(
        final_kernel,
        out_shape=jax.ShapeDtypeStruct(stream.shape, BF16),
        compiler_params=pltpu.CompilerParams(vmem_limit_bytes=32 << 20),
        name="finish",
    )(stream, parts)


def scatter_kernel(a_ref, a_out, send, recv, local):
    c, e = lax.axis_index("ctx"), lax.axis_index("ep")
    group = [
        (device(c, e, dy=dy, mirror=side), slot_of(dy, side), slot_of(-dy, side))
        for dy, side in GROUP
    ]
    greet([to for to, _, _ in group])
    own = pltpu.make_async_copy(a_ref.at[0], a_out.at[0], local)
    own.start()
    copies = []
    for to, src, dst in group:
        copies.append(remote(a_ref.at[src], a_out.at[dst], send.at[dst], recv.at[dst], *to))
        copies[-1].start()
    for copy in copies:
        copy.wait()
    own.wait()


def group_scatter(rows):
    return pl.pallas_call(
        scatter_kernel,
        out_shape=jax.ShapeDtypeStruct(rows.shape, rows.dtype),
        in_specs=[ANY],
        out_specs=ANY,
        scratch_shapes=[
            pltpu.SemaphoreType.DMA((8,)),
            pltpu.SemaphoreType.DMA((8,)),
            pltpu.SemaphoreType.DMA,
        ],
        compiler_params=params(5),
        name="group_scatter",
    )(rows)


def away(i):
    half = (i + 1) // 2
    return half * (2 * (i % 2) - 1)


def expert_kernel(
    rows_ref,
    own_wg,
    own_wu,
    own_wd,
    moved_wg,
    moved_wu,
    back_ref,
    xs,
    ps,
    from_core,
    from_side,
    sums,
    done,
    wg,
    wu,
    wd,
    z_send,
    z_recv,
    x_send,
    x_recv,
    s_send,
    s_recv,
    c_send,
    c_recv,
    f_send,
    f_recv,
    b_send,
    b_recv,
    w_send,
    w_recv,
    local,
):
    c, e = lax.axis_index("ctx"), lax.axis_index("ep")
    z, x = c // 2, c % 2
    side, other = z * 2 + (1 - x), e + 1 - 2 * (e % 2)
    n = 8
    moved = (z % 2) != (e % 2)
    diagonal = (c + 2 - 4 * (z % 2), other)
    swap = remote(own_wd, wd, w_send, w_recv, *diagonal)

    def load(refs):
        copies = []
        for i, (src, dst) in enumerate(zip(refs, (wg, wu, wd))):
            copies.append(pltpu.make_async_copy(src, dst, local.at[i]))
        return copies

    @pl.when(moved)
    def _():
        for copy in load((moved_wg, moved_wu)):
            copy.start()

    @pl.when(jnp.logical_not(moved))
    def _():
        for copy in load((own_wg, own_wu, own_wd)):
            copy.start()

    own = pltpu.make_async_copy(rows_ref.at[0], xs.at[0, 0], local.at[3])
    own.start()
    peers = [(((z + d) % n) * 2 + x, e) for d in range(1, n)]
    greet(peers + [(side, e), (c, other), diagonal])

    def out(i):
        to = ((z + n - away(i)) % n) * 2 + x
        return remote(rows_ref.at[i], xs.at[i, 0], z_send.at[i], z_recv.at[i], to, e)

    def to_side(i):
        return remote(xs.at[i, 0], xs.at[i, 1], x_send.at[i], x_recv.at[i], side, e)

    def to_core(i, q):
        return remote(
            xs.at[i, q], xs.at[i, q + 2], s_send.at[i, q], s_recv.at[i, q], c, other
        )

    def sum_core(i):
        return remote(
            ps.at[i, pl.ds(2, 2)], from_core.at[i], c_send.at[i], c_recv.at[i], c, other
        )

    def sum_side(i):
        return remote(
            sums.at[i], from_side.at[i], f_send.at[i], f_recv.at[i], side, e
        )

    def home(i):
        to = ((z + n + away(i)) % n) * 2 + x
        return remote(done.at[i], back_ref.at[i], b_send.at[i], b_recv.at[i], to, e)

    for i in range(1, WINDOW + 1):
        out(i).start()

    @pl.when(moved)
    def _():
        swap.start()

    own.wait()
    for copy in load((own_wg, own_wu)):
        copy.wait()

    def step(s, carry):
        @pl.when(s < n)
        def _():
            @pl.when(s > 0)
            def _():
                out(s).wait_recv()

            @pl.when((s > 0) & (s + WINDOW < n))
            def _():
                out(s + WINDOW).start()

            to_side(s).start()
            to_core(s, 0).start()

        @pl.when((s >= 1) & (s < n + 1))
        def _():
            i = s - 1
            to_side(i).wait_recv()
            to_core(i, 1).start()

        @pl.when((s >= 2) & (s < n + 2))
        def _():
            i = s - 2

            @pl.when((s == 2) & moved)
            def _():
                swap.wait_recv()

            @pl.when((s == 2) & jnp.logical_not(moved))
            def _():
                pltpu.make_async_copy(own_wd, wd, local.at[2]).wait()

            to_core(i, 0).wait_recv()
            to_core(i, 1).wait_recv()
            shape = xs.shape[1:]
            rows = xs[i].reshape(shape[0] * shape[1], shape[2])
            dims = (((1,), (1,)), ((), ()))
            gate = lax.dot_general(rows, wg[...], dims, preferred_element_type=F32)
            upper = lax.dot_general(rows, wu[...], dims, preferred_element_type=F32)
            act = (gate / (1.0 + jnp.exp(-gate)) * upper).astype(BF16)
            part = jnp.dot(act, wd[...], preferred_element_type=F32)
            ps[i] = part.astype(BF16).reshape(shape)
            sum_core(i).start()

        @pl.when((s >= 3) & (s < n + 3))
        def _():
            i = s - 3
            sum_core(i).wait_recv()
            sums[i] = (ps[i, 1].astype(F32) + from_core[i, 1].astype(F32)).astype(BF16)
            sum_side(i).start()

        @pl.when(s >= 4)
        def _():
            i = s - 4
            sum_side(i).wait_recv()
            done[i] = (
                ps[i, 0].astype(F32) + from_core[i, 0].astype(F32) + from_side[i].astype(F32)
            ).astype(BF16)

            @pl.when(i > 0)
            def _():
                home(i).start()

        return carry

    lax.fori_loop(0, n + 4, step, 0)
    last = pltpu.make_async_copy(done.at[0], back_ref.at[0], local.at[3])
    last.start()

    def drain(i, carry):
        to_side(i).wait_send()
        to_core(i, 0).wait_send()
        to_core(i, 1).wait_send()
        sum_core(i).wait_send()
        sum_side(i).wait_send()

        @pl.when(i > 0)
        def _():
            out(i).wait_send()
            home(i).wait()

        return carry

    lax.fori_loop(0, n, drain, 0)

    @pl.when(moved)
    def _():
        swap.wait_send()

    last.wait()


def experts(rows, own, moved):
    wg, wu, wd = own
    n, cap, width = rows.shape
    dma = pltpu.SemaphoreType.DMA
    return pl.pallas_call(
        expert_kernel,
        out_shape=jax.ShapeDtypeStruct(rows.shape, BF16),
        in_specs=[ANY] * 6,
        out_specs=ANY,
        scratch_shapes=[
            pltpu.VMEM((n, 4, cap, width), BF16),
            pltpu.VMEM((n, 4, cap, width), BF16),
            pltpu.VMEM((n, 2, cap, width), BF16),
            pltpu.VMEM((n, cap, width), BF16),
            pltpu.VMEM((n, cap, width), BF16),
            pltpu.VMEM((n, cap, width), BF16),
            pltpu.VMEM(wg.shape, BF16),
            pltpu.VMEM(wu.shape, BF16),
            pltpu.VMEM(wd.shape, BF16),
            dma((n,)),
            dma((n,)),
            dma((n,)),
            dma((n,)),
            dma((n, 2)),
            dma((n, 2)),
            dma((n,)),
            dma((n,)),
            dma((n,)),
            dma((n,)),
            dma((n,)),
            dma((n,)),
            dma,
            dma,
            dma((4,)),
        ],
        compiler_params=params(3),
        name="experts",
    )(rows, *own, *moved)


def body(
    queries,
    keys,
    values,
    segments,
    residual,
    out_weight,
    norm_gain,
    router,
    routes,
    gate_weight,
    up_weight,
    down_weight,
):
    tok, width = residual.shape
    own = (gate_weight[0, 0].T, up_weight[0, 0].T, down_weight[0, 0])
    padded = jnp.pad(routes, ((0, 0), (0, 128 - routes.shape[1])), constant_values=-1)
    stream, rows, weights, *moved = front(
        queries,
        keys,
        values,
        segments,
        out_weight,
        residual,
        norm_gain,
        padded,
        router.T,
        own[:2],
    )
    slots = 8 * CAP
    back = experts(rows.reshape(8, slots, width), own, moved)
    mixed = combine(weights, back.reshape(8 * slots, width))
    parts = group_scatter(mixed.reshape(8, tok, width))
    return finish(stream, parts)


def solution(mesh):
    placed = (
        P("ctx", "ep"),
        P("ctx", "ep"),
        P("ctx", "ep"),
        P(),
        P(("ctx", "ep"), None),
        P("ep", None),
        P(),
        P(),
        P(("ctx", "ep"), None),
        P("ep", "ctx", None, None),
        P("ep", "ctx", None, None),
        P("ep", "ctx", None, None),
    )
    return jax.shard_map(
        body, mesh=mesh, in_specs=placed, out_specs=P(("ctx", "ep"), None), check_vma=False
    )
```

```python
import jax
import jax.numpy as jnp
from jax import lax
from jax.experimental import pallas as pl
from jax.experimental.pallas import tpu as pltpu
from jax.sharding import PartitionSpec as P

HD = 128
CAP = 6
WINDOW = 2
MESH = pl.DeviceIdType.MESH
ANY = pl.BlockSpec(memory_space=pl.ANY)
BF16 = jnp.bfloat16
F32 = jnp.float32
LOG2E = 1.4426950408889634


def remote(src, dst, send, recv, ctx, ep):
    return pltpu.make_async_remote_copy(
        src_ref=src,
        dst_ref=dst,
        send_sem=send,
        recv_sem=recv,
        device_id=(ctx, ep),
        device_id_type=MESH,
    )


def greet(peers):
    barrier = pltpu.get_barrier_semaphore()
    for ctx, ep in peers:
        pl.semaphore_signal(barrier, inc=1, device_id=(ctx, ep), device_id_type=MESH)
    pl.semaphore_wait(barrier, len(peers))


def params(collective_id, vmem=60 << 20):
    return pltpu.CompilerParams(
        collective_id=collective_id, has_side_effects=True, vmem_limit_bytes=vmem
    )


def device(c, e, dz=0, dy=0, mirror=False):
    z, x, y, x_hi, core = c // 2, c % 2, e // 4, (e // 2) % 2, e % 2
    if mirror:
        x, x_hi = 1 - x, 1 - x_hi
    return ((z + dz + 8) % 8) * 2 + x, ((y + dy + 4) % 4) * 4 + x_hi * 2 + core


GROUP = [(dy, side) for dy in range(4) for side in (False, True)][1:]


def slot_of(dy, side):
    return ((dy + 4) % 4) * 2 + int(side)


def front_kernel(
    q_ref,
    k_ref,
    v_ref,
    seg_ref,
    w_ref,
    res_ref,
    gain_ref,
    route_ref,
    router_ref,
    own_wg,
    own_wu,
    own_wd,
    stream_ref,
    rows_ref,
    weight_ref,
    moved_wg,
    moved_wu,
    moved_wd,
    kv,
    queries,
    away_acc,
    away_stat,
    there_acc,
    there_stat,
    w,
    att,
    heads,
    normed,
    tok_ref,
    routes_ref,
    best,
    total,
    acc,
    kv_send,
    kv_recv,
    w_send,
    w_recv,
    h_send,
    h_recv,
    r_send,
    r_recv,
    t_send,
    t_recv,
    m_send,
    m_recv,
):
    c, e = lax.axis_index("ctx"), lax.axis_index("ep")
    z, x = c // 2, c % 2
    ox = 1 - x
    tok = res_ref.shape[0]
    rows = q_ref.shape[0]
    per = rows // 128
    scale = (HD**-0.5) * LOG2E
    up, down, side = (((z + 1) % 8) * 2 + x, e), (((z + 7) % 8) * 2 + x, e), (z * 2 + ox, e)
    north, south = device(c, e, dy=1), device(c, e, dy=-1)
    across = device(c, e, mirror=True)
    sibling = (c, e + 1 - 2 * (e % 2))
    diagonal = (c + 2 - 4 * (z % 2), e + 1 - 2 * (e % 2))
    everyone = [(c, (e + d) % 16) for d in range(1, 16)]
    everyone += [device(c, e, dy=dy, mirror=True) for dy in range(4)]
    greet(everyone + [up, down, side, diagonal])
    started = []

    def line(send, recv):
        count = [0]

        def go(src, dst, to):
            i = count[0]
            count[0] += 1
            copy = remote(src, dst, send.at[i], recv.at[i], *to)
            copy.start()
            started.append(copy)
            return copy

        return go

    go = line(kv_send, kv_recv)
    go_w = line(w_send, w_recv)
    go_r = line(r_send, r_recv)
    go_t = line(t_send, t_recv)

    kv[z, 0] = k_ref[...]
    kv[z, 1] = v_ref[...]
    away_stat[...] = jnp.zeros_like(away_stat)
    ask = go(q_ref, queries.at[1], side)
    ups = {1: go(kv.at[z], kv.at[z], up)}
    downs = {1: go(kv.at[z], kv.at[z], down)}
    queries[0] = q_ref[...]

    w[e] = w_ref[...]
    half = w_ref.shape[0] // 2
    own_up = go_w(w.at[e], w.at[e], north)
    own_down = go_w(w.at[e], w.at[e], south)
    crossing = go_w(w.at[e], w.at[e], across)
    shared = [go_w(w.at[e], w.at[e], sibling)]
    e_across = across[1]

    def at_y(base, dy):
        return ((base // 4 + dy + 4) % 4) * 4 + base % 4

    routes = [
        go_r(route_ref, routes_ref.at[slot_of(-dy, far)], device(c, e, dy=dy, mirror=far))
        for dy, far in GROUP
    ]
    routes_ref[0] = route_ref[...]

    moved = (z % 2) != (e % 2)
    halves = own_wg.shape[0] // 2
    swap = []
    for src, dst in ((own_wg, moved_wg), (own_wu, moved_wu), (own_wd, moved_wd)):
        for at in (pl.ds(0, halves), pl.ds(halves, halves)):
            i = len(swap)
            swap.append(
                remote(src.at[at], dst.at[at], m_send.at[i], m_recv.at[i], *diagonal)
            )

    def push(*pieces):
        @pl.when(moved)
        def _():
            for i in pieces:
                swap[i].start()

    def seg_row(block):
        parts = [seg_ref[pl.ds(block * per + i, 1), :] for i in range(per)]
        return jnp.concatenate(parts, axis=1)

    ids = jnp.concatenate([seg_row(c), seg_row(side[0])], axis=1)
    below_1 = jnp.sum(jnp.where(seg_ref[...] < 1, 1, 0), keepdims=True)
    below_2 = jnp.sum(jnp.where(seg_ref[...] < 2, 1, 0), keepdims=True)
    start = jnp.where(ids < 1, 0, jnp.where(ids < 2, below_1, below_2))

    def scores(plane):
        s = lax.dot_general(
            kv[plane, 0],
            queries[...].reshape(2 * rows, HD),
            (((1,), (1,)), ((), ())),
            preferred_element_type=F32,
        )
        key = lax.broadcasted_iota(jnp.int32, s.shape, 0)
        return s, key, key >= start - (plane * 2 + x) * rows

    def mix(plane, p):
        return lax.dot_general(
            kv[plane, 1],
            p.astype(BF16),
            (((0,), (0,)), ((), ())),
            preferred_element_type=F32,
        )

    def tile(plane, wanted):
        @pl.when(wanted)
        def _():
            s, _, same = scores(plane)
            s = jnp.where(same, s, -1e30)
            old = best[...]
            new = jnp.maximum(old, jnp.max(s, axis=0, keepdims=True))
            p = jnp.exp2((s - new) * scale)
            factor = jnp.exp2((old - new) * scale)
            best[...] = new
            total[...] = total[...] * factor + jnp.sum(p, axis=0, keepdims=True)
            acc[...] = acc[...] * factor + mix(plane, p)

    ask.wait_recv()
    s, key, same = scores(z)
    lane = lax.broadcasted_iota(jnp.int32, (1, 2 * rows), 1)
    reach = jnp.where(lane < rows, lane, jnp.where(x == 0, rows, -1))
    s = jnp.where(same & (key <= reach), s, -1e30)
    new = jnp.maximum(jnp.max(s, axis=0, keepdims=True), -1e29)
    p = jnp.exp2((s - new) * scale)
    best[...] = new
    total[...] = jnp.sum(p, axis=0, keepdims=True)
    acc[...] = mix(z, p)

    for t in range(1, 5):
        below, above = (z + 8 - t) % 8, (z + t) % 8
        ups[t].wait_recv()
        if t <= 2:
            ups[t + 1] = go(kv.at[below], kv.at[below], up)
        elif t == 3:
            ups[4] = go(kv.at[below, 0], kv.at[below, 0], up)
        downs[t].wait_recv()
        if t <= 2:
            downs[t + 1] = go(kv.at[above], kv.at[above], down)
        elif t == 3:
            downs[4] = go(kv.at[above, 1], kv.at[above, 1], down)

            push(1, 2)

        if t == 2:
            push(0)
            crossing.wait_recv()
            far_up = go_w(w.at[e_across], w.at[e_across], north)
            far_down = go_w(w.at[e_across], w.at[e_across], south)
            shared.append(go_w(w.at[e_across], w.at[e_across], sibling))
        tile(below, z >= t)
        if t <= 3:
            tile(above, z + t >= 8)
        if t == 2 or t == 4:
            base = e if t == 2 else e_across
            (own_up if t == 2 else far_up).wait_recv()
            here = w.at[at_y(base, -1), pl.ds(0, half)]
            second_up = go_w(here, here, north)
            here = w.at[at_y(base, -1)]
            shared.append(go_w(here, here, sibling))
            (own_down if t == 2 else far_down).wait_recv()
            here = w.at[at_y(base, 1), pl.ds(half, half)]
            second_down = go_w(here, here, south)
            here = w.at[at_y(base, 1)]
            shared.append(go_w(here, here, sibling))
            if t == 2:
                seconds = [(second_up, second_down, e)]
            else:
                seconds.append((second_up, second_down, e_across))
        if t == 4:
            away_acc[...] = acc[:, rows : 2 * rows].astype(BF16)
            away_stat[0:1, :] = best[:, rows : 2 * rows]
            away_stat[1:2, :] = total[:, rows : 2 * rows]
            give_acc = go(away_acc, there_acc, side)
            give_stat = go(away_stat, there_stat, side)
    give_acc.wait_recv()
    give_stat.wait_recv()
    b0, b1 = best[:, 0:rows], there_stat[0:1, :]
    new = jnp.maximum(b0, b1)
    f0, f1 = jnp.exp2((b0 - new) * scale), jnp.exp2((b1 - new) * scale)
    whole = total[:, 0:rows] * f0 + there_stat[1:2, :] * f1
    mixed = (acc[:, 0:rows] * f0 + there_acc[...].astype(F32) * f1) / whole
    att[...] = mixed.T.astype(BF16)

    def mine(of):
        return pl.ds(pl.multiple_of(of * tok, tok), tok)

    arrivals = []
    for d in range(1, 16):
        to = (e + d) % 16
        copy = remote(att.at[mine(to)], heads.at[e], h_send.at[d], h_recv.at[d], c, to)
        copy.start()
        started.append(copy)
        arrivals.append(copy)
    heads[e] = att[mine(e), :]
    push(3)
    for second_up, second_down, base in seconds:
        second_up.wait_recv()
        second_down.wait_recv()
        here = w.at[at_y(base, 2)]
        shared.append(go_w(here, here, sibling))
    for copy in arrivals:
        copy.wait_recv()
    for copy in shared:
        copy.wait_recv()

    push(4)
    wide = jnp.concatenate([heads[h] for h in range(16)], axis=1)
    s = res_ref[...].astype(F32) + jnp.dot(
        wide, w[...].reshape(wide.shape[1], -1), preferred_element_type=F32
    )
    stream_ref[...] = s
    mean = jnp.mean(s * s, axis=1, keepdims=True)
    normed[...] = (s * lax.rsqrt(mean + 1e-06) * gain_ref[...]).astype(BF16)

    lower, upper = pl.ds(0, tok // 2), pl.ds(tok // 2, tok // 2)
    crossing = go_t(normed, tok_ref.at[1], across)
    arrive_up = [go_t(normed, tok_ref.at[slot_of(-1, 0)], north)]
    arrive_down = [go_t(normed, tok_ref.at[slot_of(1, 0)], south)]
    tok_ref[0] = normed[...]
    push(5)
    crossing.wait_recv()
    arrive_up.append(go_t(tok_ref.at[1], tok_ref.at[slot_of(-1, 1)], north))
    arrive_down.append(go_t(tok_ref.at[1], tok_ref.at[slot_of(1, 1)], south))
    last = []
    for far in (0, 1):
        arrive_up[far].wait_recv()
        here, there = tok_ref.at[slot_of(-1, far)], tok_ref.at[slot_of(2, far)]
        last.append(go_t(here.at[lower], there.at[lower], north))
        arrive_down[far].wait_recv()
        here = tok_ref.at[slot_of(1, far)]
        last.append(go_t(here.at[upper], there.at[upper], south))
    for copy in last + routes:
        copy.wait_recv()
    tokens = tok_ref[...].reshape(8 * tok, tok_ref.shape[2])
    chosen, weights = placement(
        z,
        8 * (e // 2),
        routes_ref[...].reshape(8 * tok, 128),
        router_ref.shape[0],
        tokens,
        router_ref[...],
    )
    rows_ref[...] = lax.dot_general(
        jnp.where(chosen, 1.0, 0.0).astype(BF16),
        tokens,
        (((0,), (0,)), ((), ())),
        preferred_element_type=F32,
    ).astype(BF16)
    weight_ref[...] = weights
    for copy in started:
        copy.wait_send()

    @pl.when(moved)
    def _():
        for copy in swap:
            copy.wait()


def front(
    queries, keys, values, segments, out_weight, residual, gain, routes, router, own
):
    rows = queries.shape[0]
    tok, width = residual.shape
    slots = 64 * CAP
    vmem = pl.BlockSpec(memory_space=pltpu.VMEM)
    dma = pltpu.SemaphoreType.DMA
    return pl.pallas_call(
        front_kernel,
        out_shape=(
            jax.ShapeDtypeStruct((tok, width), F32),
            jax.ShapeDtypeStruct((slots, width), BF16),
            jax.ShapeDtypeStruct((8 * tok, slots), F32),
            *[jax.ShapeDtypeStruct(w.shape, w.dtype) for w in own],
        ),
        in_specs=[vmem] * 9 + [ANY] * 3,
        out_specs=(vmem, vmem, vmem, ANY, ANY, ANY),
        scratch_shapes=[
            pltpu.VMEM((8, 2, rows, HD), BF16),
            pltpu.VMEM((2, rows, HD), BF16),
            pltpu.VMEM((HD, rows), BF16),
            pltpu.VMEM((8, rows), F32),
            pltpu.VMEM((HD, rows), BF16),
            pltpu.VMEM((8, rows), F32),
            pltpu.VMEM((16,) + out_weight.shape, BF16),
            pltpu.VMEM((rows, HD), BF16),
            pltpu.VMEM((16, tok, HD), BF16),
            pltpu.VMEM((tok, width), BF16),
            pltpu.VMEM((8, tok, width), BF16),
            pltpu.VMEM((8,) + routes.shape, jnp.int32),
            pltpu.VMEM((1, 2 * rows), F32),
            pltpu.VMEM((1, 2 * rows), F32),
            pltpu.VMEM((HD, 2 * rows), F32),
            dma((11,)),
            dma((11,)),
            dma((18,)),
            dma((18,)),
            dma((16,)),
            dma((16,)),
            dma((7,)),
            dma((7,)),
            dma((9,)),
            dma((9,)),
            dma((6,)),
            dma((6,)),
        ],
        compiler_params=params(1),
        name="front",
    )(
        queries,
        keys,
        values,
        segments.reshape(-1, 128),
        out_weight,
        residual,
        gain.reshape(1, width),
        routes,
        router,
        *own,
    )


def placement(z, first, routes, experts, tokens, router):
    count = routes.shape[0]
    slots = 8 * CAP
    width = 8 * slots
    ids = lax.broadcasted_iota(jnp.int32, (count, experts), 1)
    named = routes[:, 0:1] == ids
    for k in range(1, 6):
        named = named | (routes[:, k : k + 1] == ids)
    named = jnp.where(named, 1.0, 0.0)
    t0 = lax.broadcasted_iota(jnp.int32, (count, count), 0)
    t1 = lax.broadcasted_iota(jnp.int32, (count, count), 1)
    before = jnp.where((t1 < t0) & ((t1 >> 5) == (t0 >> 5)), 1.0, 0.0).astype(BF16)
    rank = jnp.dot(before, named.astype(BF16), preferred_element_type=F32)
    owner = lax.broadcasted_iota(jnp.int32, (count, experts), 0) >> 5
    place = jnp.where(named > 0, rank + (owner * CAP).astype(F32), -1.0)
    col = lax.broadcasted_iota(jnp.int32, (experts, width), 1)
    block = jnp.zeros_like(col)
    for k in range(1, 8):
        block = block + jnp.where(col >= k * slots, 1, 0)
    turn = (8 - block) & 7
    at = (z + 8 - ((turn + 1) >> 1) * (2 * (turn & 1) - 1)) & 7
    expert = first + 4 * (at & 1) + (at >> 1)
    pick = jnp.where(
        lax.broadcasted_iota(jnp.int32, (experts, width), 0) == expert, 1.0, 0.0
    ).astype(BF16)
    spread = jnp.dot(place.astype(BF16), pick, preferred_element_type=F32)
    chosen = spread == (col[0:1, :] - slots * block[0:1, :]).astype(F32)
    high = router.astype(BF16)
    low = (router - high.astype(F32)).astype(BF16)
    dims = (((1,), (1,)), ((), ()))
    logits = lax.dot_general(
        tokens, high, dims, preferred_element_type=F32
    ) + lax.dot_general(tokens, low, dims, preferred_element_type=F32)
    gates = named * jax.nn.sigmoid(logits)
    weights = gates / jnp.sum(gates, axis=1, keepdims=True)
    high = weights.astype(BF16)
    low = (weights - high.astype(F32)).astype(BF16)
    spread = jnp.dot(high, pick, preferred_element_type=F32) + jnp.dot(
        low, pick, preferred_element_type=F32
    )
    return chosen, jnp.where(chosen, spread, 0.0)


def away(i):
    i = (8 - i) % 8
    half = (i + 1) // 2
    return half * (2 * (i % 2) - 1)


def expert_kernel(
    rows_ref,
    own_wg,
    own_wu,
    own_wd,
    moved_wg,
    moved_wu,
    moved_wd,
    weight_ref,
    stream_ref,
    out_ref,
    back_ref,
    parts,
    got,
    xs,
    ps,
    from_core,
    from_side,
    sums,
    done,
    wg,
    wu,
    wd,
    z_send,
    z_recv,
    x_send,
    x_recv,
    s_send,
    s_recv,
    c_send,
    c_recv,
    f_send,
    f_recv,
    b_send,
    b_recv,
    p_send,
    p_recv,
    local,
):
    c, e = lax.axis_index("ctx"), lax.axis_index("ep")
    z, x = c // 2, c % 2
    side, other = z * 2 + (1 - x), e + 1 - 2 * (e % 2)
    n = 8
    moved = (z % 2) != (e % 2)

    def load(refs):
        copies = []
        for i, (src, dst) in enumerate(zip(refs, (wg, wu, wd))):
            copies.append(pltpu.make_async_copy(src, dst, local.at[i]))
        return copies

    @pl.when(moved)
    def _():
        for copy in load((moved_wg, moved_wu, moved_wd)):
            copy.start()

    @pl.when(jnp.logical_not(moved))
    def _():
        for copy in load((own_wg, own_wu, own_wd)):
            copy.start()

    own = pltpu.make_async_copy(rows_ref.at[0], xs.at[0, 0], local.at[3])
    own.start()
    peers = [(((z + d) % n) * 2 + x, e) for d in range(1, n)]
    group = [
        (device(c, e, dy=dy, mirror=far), slot_of(dy, far), slot_of(-dy, far))
        for dy, far in GROUP
    ]
    greet(peers + [(side, e), (c, other)] + [to for to, _, _ in group])

    def out(i):
        to = ((z + n - away(i)) % n) * 2 + x
        return remote(rows_ref.at[i], xs.at[i, 0], z_send.at[i], z_recv.at[i], to, e)

    def to_side(i):
        return remote(xs.at[i, 0], xs.at[i, 1], x_send.at[i], x_recv.at[i], side, e)

    def to_core(i, q):
        return remote(
            xs.at[i, q], xs.at[i, q + 2], s_send.at[i, q], s_recv.at[i, q], c, other
        )

    def sum_core(i):
        return remote(
            ps.at[i, pl.ds(2, 2)], from_core.at[i], c_send.at[i], c_recv.at[i], c, other
        )

    def sum_side(i):
        return remote(
            sums.at[i], from_side.at[i], f_send.at[i], f_recv.at[i], side, e
        )

    def home(i):
        to = ((z + n + away(i)) % n) * 2 + x
        return remote(done.at[i], back_ref.at[i], b_send.at[i], b_recv.at[i], to, e)

    for i in range(1, WINDOW + 1):
        out(i).start()

    own.wait()
    for copy in load((own_wg, own_wu, own_wd)):
        copy.wait()

    def step(s, carry):
        @pl.when(s < n)
        def _():
            @pl.when(s > 0)
            def _():
                out(s).wait_recv()

            @pl.when((s > 0) & (s + WINDOW < n))
            def _():
                out(s + WINDOW).start()

            to_side(s).start()
            to_core(s, 0).start()

        @pl.when((s >= 1) & (s < n + 1))
        def _():
            i = s - 1
            to_side(i).wait_recv()
            to_core(i, 1).start()

        @pl.when((s >= 3) & (s < n + 3))
        def _():
            i = s - 3
            sum_core(i).wait_recv()
            sums[i] = (ps[i, 1].astype(F32) + from_core[i, 1].astype(F32)).astype(BF16)
            sum_side(i).start()

        @pl.when(s >= 4)
        def _():
            i = s - 4
            sum_side(i).wait_recv()
            done[i] = (
                ps[i, 0].astype(F32) + from_core[i, 0].astype(F32) + from_side[i].astype(F32)
            ).astype(BF16)

            @pl.when(i > 0)
            def _():
                home(i).start()

        @pl.when((s >= 2) & (s < n + 2))
        def _():
            i = s - 2

            to_core(i, 0).wait_recv()
            to_core(i, 1).wait_recv()
            shape = xs.shape[1:]
            rows = xs[i].reshape(shape[0] * shape[1], shape[2])
            dims = (((1,), (1,)), ((), ()))
            gate = lax.dot_general(rows, wg[...], dims, preferred_element_type=F32)
            upper = lax.dot_general(rows, wu[...], dims, preferred_element_type=F32)
            act = (gate / (1.0 + jnp.exp(-gate)) * upper).astype(BF16)
            part = jnp.dot(act, wd[...], preferred_element_type=F32)
            ps[i] = part.astype(BF16).reshape(shape)
            sum_core(i).start()

        return carry

    lax.fori_loop(0, n + 4, step, 0)
    back_ref[0] = done[0]

    def arrive(i, carry):
        home(i).wait_recv()
        return carry

    lax.fori_loop(1, n, arrive, 0)
    weights = weight_ref[...]
    high = weights.astype(BF16)
    low = (weights - high.astype(F32)).astype(BF16)
    rows = back_ref[...].reshape(-1, back_ref.shape[2])
    mixed = jnp.dot(high, rows, preferred_element_type=F32) + jnp.dot(
        low, rows, preferred_element_type=F32
    )
    parts[...] = mixed.astype(BF16).reshape(parts.shape)
    copies = []
    for to, src, dst in group:
        copies.append(
            remote(parts.at[src], got.at[dst], p_send.at[dst], p_recv.at[dst], *to)
        )
        copies[-1].start()
    total = stream_ref[...] + parts[0].astype(F32)

    def drain(i, carry):
        to_side(i).wait_send()
        to_core(i, 0).wait_send()
        to_core(i, 1).wait_send()
        sum_core(i).wait_send()
        sum_side(i).wait_send()

        @pl.when(i > 0)
        def _():
            out(i).wait_send()
            home(i).wait_send()

        return carry

    lax.fori_loop(0, n, drain, 0)
    for copy in copies:
        copy.wait_recv()
    for m in range(1, 8):
        total = total + got[m].astype(F32)
    out_ref[...] = total.astype(BF16)
    for copy in copies:
        copy.wait_send()


def experts(rows, own, moved, weights, stream):
    wg, wu, wd = own
    n, cap, width = rows.shape
    dma = pltpu.SemaphoreType.DMA
    return pl.pallas_call(
        expert_kernel,
        out_shape=jax.ShapeDtypeStruct(stream.shape, BF16),
        in_specs=[ANY] * 7 + [pl.BlockSpec(memory_space=pltpu.VMEM)] * 2,
        out_specs=pl.BlockSpec(memory_space=pltpu.VMEM),
        scratch_shapes=[
            pltpu.VMEM((n, cap, width), BF16),
            pltpu.VMEM((8,) + stream.shape, BF16),
            pltpu.VMEM((8,) + stream.shape, BF16),
            pltpu.VMEM((n, 4, cap, width), BF16),
            pltpu.VMEM((n, 4, cap, width), BF16),
            pltpu.VMEM((n, 2, cap, width), BF16),
            pltpu.VMEM((n, cap, width), BF16),
            pltpu.VMEM((n, cap, width), BF16),
            pltpu.VMEM((n, cap, width), BF16),
            pltpu.VMEM(wg.shape, BF16),
            pltpu.VMEM(wu.shape, BF16),
            pltpu.VMEM(wd.shape, BF16),
            dma((n,)),
            dma((n,)),
            dma((n,)),
            dma((n,)),
            dma((n, 2)),
            dma((n, 2)),
            dma((n,)),
            dma((n,)),
            dma((n,)),
            dma((n,)),
            dma((n,)),
            dma((n,)),
            dma((8,)),
            dma((8,)),
            dma((4,)),
        ],
        compiler_params=params(3),
        name="experts",
    )(rows, *own, *moved, weights, stream)


def body(
    queries,
    keys,
    values,
    segments,
    residual,
    out_weight,
    norm_gain,
    router,
    routes,
    gate_weight,
    up_weight,
    down_weight,
):
    tok, width = residual.shape
    own = (gate_weight[0, 0].T, up_weight[0, 0].T, down_weight[0, 0])
    padded = jnp.pad(routes, ((0, 0), (0, 128 - routes.shape[1])), constant_values=-1)
    stream, rows, weights, *moved = front(
        queries,
        keys,
        values,
        segments,
        out_weight,
        residual,
        norm_gain,
        padded,
        router.T,
        own,
    )
    return experts(rows.reshape(8, 8 * CAP, width), own, moved, weights, stream)


def solution(mesh):
    placed = (
        P("ctx", "ep"),
        P("ctx", "ep"),
        P("ctx", "ep"),
        P(),
        P(("ctx", "ep"), None),
        P("ep", None),
        P(),
        P(),
        P(("ctx", "ep"), None),
        P("ep", "ctx", None, None),
        P("ep", "ctx", None, None),
        P("ep", "ctx", None, None),
    )
    return jax.shard_map(
        body, mesh=mesh, in_specs=placed, out_specs=P(("ctx", "ep"), None), check_vma=False
    )
```

```python
import jax
import jax.numpy as jnp
from jax import lax
from jax.experimental import pallas as pl
from jax.experimental.pallas import tpu as pltpu
from jax.sharding import PartitionSpec as P

HD = 128
CAP = 6
WINDOW = 2
MESH = pl.DeviceIdType.MESH
ANY = pl.BlockSpec(memory_space=pl.ANY)
BF16 = jnp.bfloat16
F32 = jnp.float32
LOG2E = 1.4426950408889634


def remote(src, dst, send, recv, ctx, ep):
    return pltpu.make_async_remote_copy(
        src_ref=src,
        dst_ref=dst,
        send_sem=send,
        recv_sem=recv,
        device_id=(ctx, ep),
        device_id_type=MESH,
    )


def greet(peers):
    barrier = pltpu.get_barrier_semaphore()
    for ctx, ep in peers:
        pl.semaphore_signal(barrier, inc=1, device_id=(ctx, ep), device_id_type=MESH)
    pl.semaphore_wait(barrier, len(peers))


def params(collective_id, vmem=60 << 20):
    return pltpu.CompilerParams(
        collective_id=collective_id, has_side_effects=True, vmem_limit_bytes=vmem
    )


def device(c, e, dz=0, dy=0, mirror=False):
    z, x, y, x_hi, core = c // 2, c % 2, e // 4, (e // 2) % 2, e % 2
    if mirror:
        x, x_hi = 1 - x, 1 - x_hi
    return ((z + dz + 8) % 8) * 2 + x, ((y + dy + 4) % 4) * 4 + x_hi * 2 + core


GROUP = [(dy, side) for dy in range(4) for side in (False, True)][1:]


def slot_of(dy, side):
    return ((dy + 4) % 4) * 2 + int(side)


def front_kernel(
    q_ref,
    k_ref,
    v_ref,
    seg_ref,
    w_ref,
    res_ref,
    gain_ref,
    route_ref,
    router_ref,
    own_wg,
    own_wu,
    own_wd,
    stream_ref,
    rows_ref,
    weight_ref,
    moved_wg,
    moved_wu,
    moved_wd,
    kv,
    queries,
    away_acc,
    away_stat,
    there_acc,
    there_stat,
    w,
    att,
    heads,
    normed,
    tok_ref,
    routes_ref,
    best,
    total,
    acc,
    kv_send,
    kv_recv,
    w_send,
    w_recv,
    h_send,
    h_recv,
    r_send,
    r_recv,
    t_send,
    t_recv,
    m_send,
    m_recv,
):
    c, e = lax.axis_index("ctx"), lax.axis_index("ep")
    z, x = c // 2, c % 2
    ox = 1 - x
    tok = res_ref.shape[0]
    rows = q_ref.shape[0]
    per = rows // 128
    scale = (HD**-0.5) * LOG2E
    up, down, side = (((z + 1) % 8) * 2 + x, e), (((z + 7) % 8) * 2 + x, e), (z * 2 + ox, e)
    north, south = device(c, e, dy=1), device(c, e, dy=-1)
    across = device(c, e, mirror=True)
    sibling = (c, e + 1 - 2 * (e % 2))
    diagonal = (c + 2 - 4 * (z % 2), e + 1 - 2 * (e % 2))
    everyone = [(c, (e + d) % 16) for d in range(1, 16)]
    everyone += [device(c, e, dy=dy, mirror=True) for dy in range(4)]
    greet(everyone + [up, down, side, diagonal])
    started = []

    def line(send, recv):
        count = [0]

        def go(src, dst, to):
            i = count[0]
            count[0] += 1
            copy = remote(src, dst, send.at[i], recv.at[i], *to)
            copy.start()
            started.append(copy)
            return copy

        return go

    go = line(kv_send, kv_recv)
    go_w = line(w_send, w_recv)
    go_r = line(r_send, r_recv)
    go_t = line(t_send, t_recv)

    kv[z, 0] = k_ref[...]
    kv[z, 1] = v_ref[...]
    away_stat[...] = jnp.zeros_like(away_stat)
    ask = go(q_ref, queries.at[1], side)
    ups = {1: go(kv.at[z], kv.at[z], up)}
    downs = {1: go(kv.at[z], kv.at[z], down)}
    queries[0] = q_ref[...]

    w[e] = w_ref[...]
    half = w_ref.shape[0] // 2
    own_up = go_w(w.at[e], w.at[e], north)
    own_down = go_w(w.at[e], w.at[e], south)
    crossing = go_w(w.at[e], w.at[e], across)
    shared = [go_w(w.at[e], w.at[e], sibling)]
    e_across = across[1]

    def at_y(base, dy):
        return ((base // 4 + dy + 4) % 4) * 4 + base % 4

    routes = [
        go_r(route_ref, routes_ref.at[slot_of(-dy, far)], device(c, e, dy=dy, mirror=far))
        for dy, far in GROUP
    ]
    routes_ref[0] = route_ref[...]

    moved = (z % 2) != (e % 2)
    halves = own_wg.shape[0] // 2
    swap = []
    for src, dst in ((own_wg, moved_wg), (own_wu, moved_wu), (own_wd, moved_wd)):
        for at in (pl.ds(0, halves), pl.ds(halves, halves)):
            i = len(swap)
            swap.append(
                remote(src.at[at], dst.at[at], m_send.at[i], m_recv.at[i], *diagonal)
            )

    def push(*pieces):
        @pl.when(moved)
        def _():
            for i in pieces:
                swap[i].start()

    def seg_row(block):
        parts = [seg_ref[pl.ds(block * per + i, 1), :] for i in range(per)]
        return jnp.concatenate(parts, axis=1)

    ids = jnp.concatenate([seg_row(c), seg_row(side[0])], axis=1)
    below_1 = jnp.sum(jnp.where(seg_ref[...] < 1, 1, 0), keepdims=True)
    below_2 = jnp.sum(jnp.where(seg_ref[...] < 2, 1, 0), keepdims=True)
    start = jnp.where(ids < 1, 0, jnp.where(ids < 2, below_1, below_2))

    def scores(plane):
        s = lax.dot_general(
            kv[plane, 0],
            queries[...].reshape(2 * rows, HD),
            (((1,), (1,)), ((), ())),
            preferred_element_type=F32,
        )
        key = lax.broadcasted_iota(jnp.int32, s.shape, 0)
        return s, key, key >= start - (plane * 2 + x) * rows

    def mix(plane, p):
        return lax.dot_general(
            kv[plane, 1],
            p.astype(BF16),
            (((0,), (0,)), ((), ())),
            preferred_element_type=F32,
        )

    def tile(plane, wanted):
        @pl.when(wanted)
        def _():
            s, _, same = scores(plane)
            s = jnp.where(same, s, -1e30)
            old = best[...]
            new = jnp.maximum(old, jnp.max(s, axis=0, keepdims=True))
            p = jnp.exp2((s - new) * scale)
            factor = jnp.exp2((old - new) * scale)
            best[...] = new
            total[...] = total[...] * factor + jnp.sum(p, axis=0, keepdims=True)
            acc[...] = acc[...] * factor + mix(plane, p)

    ask.wait_recv()
    s, key, same = scores(z)
    lane = lax.broadcasted_iota(jnp.int32, (1, 2 * rows), 1)
    reach = jnp.where(lane < rows, lane, jnp.where(x == 0, rows, -1))
    s = jnp.where(same & (key <= reach), s, -1e30)
    new = jnp.maximum(jnp.max(s, axis=0, keepdims=True), -1e29)
    p = jnp.exp2((s - new) * scale)
    best[...] = new
    total[...] = jnp.sum(p, axis=0, keepdims=True)
    acc[...] = mix(z, p)

    for t in range(1, 5):
        below, above = (z + 8 - t) % 8, (z + t) % 8
        ups[t].wait_recv()
        if t <= 2:
            ups[t + 1] = go(kv.at[below], kv.at[below], up)
        elif t == 3:
            ups[4] = go(kv.at[below, 0], kv.at[below, 0], up)
        downs[t].wait_recv()
        if t <= 2:
            downs[t + 1] = go(kv.at[above], kv.at[above], down)
        elif t == 3:
            downs[4] = go(kv.at[above, 1], kv.at[above, 1], down)

            push(2, 3)

        if t <= 2:
            push(t - 1)
        if t == 2:
            crossing.wait_recv()
            far_up = go_w(w.at[e_across], w.at[e_across], north)
            far_down = go_w(w.at[e_across], w.at[e_across], south)
            shared.append(go_w(w.at[e_across], w.at[e_across], sibling))
        tile(below, z >= t)
        if t <= 3:
            tile(above, z + t >= 8)
        if t == 2 or t == 4:
            base = e if t == 2 else e_across
            (own_up if t == 2 else far_up).wait_recv()
            here = w.at[at_y(base, -1), pl.ds(0, half)]
            second_up = go_w(here, here, north)
            here = w.at[at_y(base, -1)]
            shared.append(go_w(here, here, sibling))
            (own_down if t == 2 else far_down).wait_recv()
            here = w.at[at_y(base, 1), pl.ds(half, half)]
            second_down = go_w(here, here, south)
            here = w.at[at_y(base, 1)]
            shared.append(go_w(here, here, sibling))
            if t == 2:
                seconds = [(second_up, second_down, e)]
            else:
                seconds.append((second_up, second_down, e_across))
        if t == 4:
            away_acc[...] = acc[:, rows : 2 * rows].astype(BF16)
            away_stat[0:1, :] = best[:, rows : 2 * rows]
            away_stat[1:2, :] = total[:, rows : 2 * rows]
            give_acc = go(away_acc, there_acc, side)
            give_stat = go(away_stat, there_stat, side)
    give_acc.wait_recv()
    give_stat.wait_recv()
    b0, b1 = best[:, 0:rows], there_stat[0:1, :]
    new = jnp.maximum(b0, b1)
    f0, f1 = jnp.exp2((b0 - new) * scale), jnp.exp2((b1 - new) * scale)
    whole = total[:, 0:rows] * f0 + there_stat[1:2, :] * f1
    mixed = (acc[:, 0:rows] * f0 + there_acc[...].astype(F32) * f1) / whole
    att[...] = mixed.T.astype(BF16)

    def mine(of):
        return pl.ds(pl.multiple_of(of * tok, tok), tok)

    arrivals = []
    for d in range(1, 16):
        to = (e + d) % 16
        copy = remote(att.at[mine(to)], heads.at[e], h_send.at[d], h_recv.at[d], c, to)
        copy.start()
        started.append(copy)
        arrivals.append(copy)
    heads[e] = att[mine(e), :]
    push(4)
    for second_up, second_down, base in seconds:
        second_up.wait_recv()
        second_down.wait_recv()
        here = w.at[at_y(base, 2)]
        shared.append(go_w(here, here, sibling))
    for copy in arrivals:
        copy.wait_recv()
    for copy in shared:
        copy.wait_recv()

    push(5)
    wide = jnp.concatenate([heads[h] for h in range(16)], axis=1)
    s = res_ref[...].astype(F32) + jnp.dot(
        wide, w[...].reshape(wide.shape[1], -1), preferred_element_type=F32
    )
    stream_ref[...] = s
    mean = jnp.mean(s * s, axis=1, keepdims=True)
    normed[...] = (s * lax.rsqrt(mean + 1e-06) * gain_ref[...]).astype(BF16)

    lower, upper = pl.ds(0, tok // 2), pl.ds(tok // 2, tok // 2)
    crossing = go_t(normed, tok_ref.at[1], across)
    arrive_up = [go_t(normed, tok_ref.at[slot_of(-1, 0)], north)]
    arrive_down = [go_t(normed, tok_ref.at[slot_of(1, 0)], south)]
    tok_ref[0] = normed[...]
    crossing.wait_recv()
    arrive_up.append(go_t(tok_ref.at[1], tok_ref.at[slot_of(-1, 1)], north))
    arrive_down.append(go_t(tok_ref.at[1], tok_ref.at[slot_of(1, 1)], south))
    last = []
    for far in (0, 1):
        arrive_up[far].wait_recv()
        here, there = tok_ref.at[slot_of(-1, far)], tok_ref.at[slot_of(2, far)]
        last.append(go_t(here.at[lower], there.at[lower], north))
        arrive_down[far].wait_recv()
        here = tok_ref.at[slot_of(1, far)]
        last.append(go_t(here.at[upper], there.at[upper], south))
    for copy in last + routes:
        copy.wait_recv()
    tokens = tok_ref[...].reshape(8 * tok, tok_ref.shape[2])
    chosen, weights = placement(
        z,
        8 * (e // 2),
        routes_ref[...].reshape(8 * tok, 128),
        router_ref.shape[0],
        tokens,
        router_ref[...],
    )
    rows_ref[...] = lax.dot_general(
        jnp.where(chosen, 1.0, 0.0).astype(BF16),
        tokens,
        (((0,), (0,)), ((), ())),
        preferred_element_type=F32,
    ).astype(BF16)
    weight_ref[...] = weights
    for copy in started:
        copy.wait_send()

    @pl.when(moved)
    def _():
        for copy in swap:
            copy.wait()


def front(
    queries, keys, values, segments, out_weight, residual, gain, routes, router, own
):
    rows = queries.shape[0]
    tok, width = residual.shape
    slots = 64 * CAP
    vmem = pl.BlockSpec(memory_space=pltpu.VMEM)
    dma = pltpu.SemaphoreType.DMA
    return pl.pallas_call(
        front_kernel,
        out_shape=(
            jax.ShapeDtypeStruct((tok, width), F32),
            jax.ShapeDtypeStruct((slots, width), BF16),
            jax.ShapeDtypeStruct((8 * tok, slots), F32),
            *[jax.ShapeDtypeStruct(w.shape, w.dtype) for w in own],
        ),
        in_specs=[vmem] * 9 + [ANY] * 3,
        out_specs=(vmem, vmem, vmem, ANY, ANY, ANY),
        scratch_shapes=[
            pltpu.VMEM((8, 2, rows, HD), BF16),
            pltpu.VMEM((2, rows, HD), BF16),
            pltpu.VMEM((HD, rows), BF16),
            pltpu.VMEM((8, rows), F32),
            pltpu.VMEM((HD, rows), BF16),
            pltpu.VMEM((8, rows), F32),
            pltpu.VMEM((16,) + out_weight.shape, BF16),
            pltpu.VMEM((rows, HD), BF16),
            pltpu.VMEM((16, tok, HD), BF16),
            pltpu.VMEM((tok, width), BF16),
            pltpu.VMEM((8, tok, width), BF16),
            pltpu.VMEM((8,) + routes.shape, jnp.int32),
            pltpu.VMEM((1, 2 * rows), F32),
            pltpu.VMEM((1, 2 * rows), F32),
            pltpu.VMEM((HD, 2 * rows), F32),
            dma((11,)),
            dma((11,)),
            dma((18,)),
            dma((18,)),
            dma((16,)),
            dma((16,)),
            dma((7,)),
            dma((7,)),
            dma((9,)),
            dma((9,)),
            dma((6,)),
            dma((6,)),
        ],
        compiler_params=params(1),
        name="front",
    )(
        queries,
        keys,
        values,
        segments.reshape(-1, 128),
        out_weight,
        residual,
        gain.reshape(1, width),
        routes,
        router,
        *own,
    )


def placement(z, first, routes, experts, tokens, router):
    count = routes.shape[0]
    slots = 8 * CAP
    width = 8 * slots
    ids = lax.broadcasted_iota(jnp.int32, (count, experts), 1)
    named = routes[:, 0:1] == ids
    for k in range(1, 6):
        named = named | (routes[:, k : k + 1] == ids)
    named = jnp.where(named, 1.0, 0.0)
    t0 = lax.broadcasted_iota(jnp.int32, (count, count), 0)
    t1 = lax.broadcasted_iota(jnp.int32, (count, count), 1)
    before = jnp.where((t1 < t0) & ((t1 >> 5) == (t0 >> 5)), 1.0, 0.0).astype(BF16)
    rank = jnp.dot(before, named.astype(BF16), preferred_element_type=F32)
    owner = lax.broadcasted_iota(jnp.int32, (count, experts), 0) >> 5
    place = jnp.where(named > 0, rank + (owner * CAP).astype(F32), -1.0)
    col = lax.broadcasted_iota(jnp.int32, (experts, width), 1)
    block = jnp.zeros_like(col)
    for k in range(1, 8):
        block = block + jnp.where(col >= k * slots, 1, 0)
    turn = (8 - block) & 7
    at = (z + 8 - ((turn + 1) >> 1) * (2 * (turn & 1) - 1)) & 7
    expert = first + 4 * (at & 1) + (at >> 1)
    pick = jnp.where(
        lax.broadcasted_iota(jnp.int32, (experts, width), 0) == expert, 1.0, 0.0
    ).astype(BF16)
    spread = jnp.dot(place.astype(BF16), pick, preferred_element_type=F32)
    chosen = spread == (col[0:1, :] - slots * block[0:1, :]).astype(F32)
    high = router.astype(BF16)
    low = (router - high.astype(F32)).astype(BF16)
    dims = (((1,), (1,)), ((), ()))
    logits = lax.dot_general(
        tokens, high, dims, preferred_element_type=F32
    ) + lax.dot_general(tokens, low, dims, preferred_element_type=F32)
    gates = named * jax.nn.sigmoid(logits)
    weights = gates / jnp.sum(gates, axis=1, keepdims=True)
    high = weights.astype(BF16)
    low = (weights - high.astype(F32)).astype(BF16)
    spread = jnp.dot(high, pick, preferred_element_type=F32) + jnp.dot(
        low, pick, preferred_element_type=F32
    )
    return chosen, jnp.where(chosen, spread, 0.0)


def away(i):
    i = (8 - i) % 8
    half = (i + 1) // 2
    return half * (2 * (i % 2) - 1)


def expert_kernel(
    rows_ref,
    own_wg,
    own_wu,
    own_wd,
    moved_wg,
    moved_wu,
    moved_wd,
    weight_ref,
    stream_ref,
    out_ref,
    back_ref,
    parts,
    got,
    xs,
    ps,
    from_core,
    from_side,
    sums,
    done,
    wg,
    wu,
    wd,
    z_send,
    z_recv,
    x_send,
    x_recv,
    s_send,
    s_recv,
    c_send,
    c_recv,
    f_send,
    f_recv,
    b_send,
    b_recv,
    p_send,
    p_recv,
    local,
):
    c, e = lax.axis_index("ctx"), lax.axis_index("ep")
    z, x = c // 2, c % 2
    side, other = z * 2 + (1 - x), e + 1 - 2 * (e % 2)
    n = 8
    moved = (z % 2) != (e % 2)

    def load(refs):
        copies = []
        for i, (src, dst) in enumerate(zip(refs, (wg, wu, wd))):
            copies.append(pltpu.make_async_copy(src, dst, local.at[i]))
        return copies

    @pl.when(moved)
    def _():
        for copy in load((moved_wg, moved_wu, moved_wd)):
            copy.start()

    @pl.when(jnp.logical_not(moved))
    def _():
        for copy in load((own_wg, own_wu, own_wd)):
            copy.start()

    own = pltpu.make_async_copy(rows_ref.at[0], xs.at[0, 0], local.at[3])
    own.start()
    peers = [(((z + d) % n) * 2 + x, e) for d in range(1, n)]
    group = [
        (device(c, e, dy=dy, mirror=far), slot_of(dy, far), slot_of(-dy, far))
        for dy, far in GROUP
    ]
    greet(peers + [(side, e), (c, other)] + [to for to, _, _ in group])

    def out(i):
        to = ((z + n - away(i)) % n) * 2 + x
        return remote(rows_ref.at[i], xs.at[i, 0], z_send.at[i], z_recv.at[i], to, e)

    def to_side(i):
        return remote(xs.at[i, 0], xs.at[i, 1], x_send.at[i], x_recv.at[i], side, e)

    def to_core(i, q):
        return remote(
            xs.at[i, q], xs.at[i, q + 2], s_send.at[i, q], s_recv.at[i, q], c, other
        )

    def sum_core(i):
        return remote(
            ps.at[i, pl.ds(2, 2)], from_core.at[i], c_send.at[i], c_recv.at[i], c, other
        )

    def sum_side(i):
        return remote(
            sums.at[i], from_side.at[i], f_send.at[i], f_recv.at[i], side, e
        )

    def home(i):
        to = ((z + n + away(i)) % n) * 2 + x
        return remote(done.at[i], back_ref.at[i], b_send.at[i], b_recv.at[i], to, e)

    for i in range(1, WINDOW + 1):
        out(i).start()

    own.wait()
    for copy in load((own_wg, own_wu, own_wd)):
        copy.wait()

    def step(s, carry):
        @pl.when(s < n)
        def _():
            @pl.when(s > 0)
            def _():
                out(s).wait_recv()

            @pl.when((s > 0) & (s + WINDOW < n))
            def _():
                out(s + WINDOW).start()

            to_side(s).start()
            to_core(s, 0).start()

        @pl.when((s >= 1) & (s < n + 1))
        def _():
            i = s - 1
            to_side(i).wait_recv()
            to_core(i, 1).start()

        @pl.when((s >= 3) & (s < n + 3))
        def _():
            i = s - 3
            sum_core(i).wait_recv()
            sums[i] = (ps[i, 1].astype(F32) + from_core[i, 1].astype(F32)).astype(BF16)
            sum_side(i).start()

        @pl.when(s >= 4)
        def _():
            i = s - 4
            sum_side(i).wait_recv()
            done[i] = (
                ps[i, 0].astype(F32) + from_core[i, 0].astype(F32) + from_side[i].astype(F32)
            ).astype(BF16)

            @pl.when(i > 0)
            def _():
                home(i).start()

        @pl.when((s >= 2) & (s < n + 2))
        def _():
            i = s - 2

            to_core(i, 0).wait_recv()
            to_core(i, 1).wait_recv()
            shape = xs.shape[1:]
            rows = xs[i].reshape(shape[0] * shape[1], shape[2])
            dims = (((1,), (1,)), ((), ()))
            gate = lax.dot_general(rows, wg[...], dims, preferred_element_type=F32)
            upper = lax.dot_general(rows, wu[...], dims, preferred_element_type=F32)
            act = (gate / (1.0 + jnp.exp(-gate)) * upper).astype(BF16)
            part = jnp.dot(act, wd[...], preferred_element_type=F32)
            ps[i] = part.astype(BF16).reshape(shape)
            sum_core(i).start()

        return carry

    lax.fori_loop(0, n + 4, step, 0)
    back_ref[0] = done[0]

    def arrive(i, carry):
        home(i).wait_recv()
        return carry

    lax.fori_loop(1, n, arrive, 0)
    weights = weight_ref[...]
    high = weights.astype(BF16)
    low = (weights - high.astype(F32)).astype(BF16)
    rows = back_ref[...].reshape(-1, back_ref.shape[2])
    mixed = jnp.dot(high, rows, preferred_element_type=F32) + jnp.dot(
        low, rows, preferred_element_type=F32
    )
    parts[...] = mixed.astype(BF16).reshape(parts.shape)
    copies = []
    for to, src, dst in group:
        copies.append(
            remote(parts.at[src], got.at[dst], p_send.at[dst], p_recv.at[dst], *to)
        )
        copies[-1].start()
    total = stream_ref[...] + parts[0].astype(F32)

    def drain(i, carry):
        to_side(i).wait_send()
        to_core(i, 0).wait_send()
        to_core(i, 1).wait_send()
        sum_core(i).wait_send()
        sum_side(i).wait_send()

        @pl.when(i > 0)
        def _():
            out(i).wait_send()
            home(i).wait_send()

        return carry

    lax.fori_loop(0, n, drain, 0)
    for copy in copies:
        copy.wait_recv()
    for m in range(1, 8):
        total = total + got[m].astype(F32)
    out_ref[...] = total.astype(BF16)
    for copy in copies:
        copy.wait_send()


def experts(rows, own, moved, weights, stream):
    wg, wu, wd = own
    n, cap, width = rows.shape
    dma = pltpu.SemaphoreType.DMA
    return pl.pallas_call(
        expert_kernel,
        out_shape=jax.ShapeDtypeStruct(stream.shape, BF16),
        in_specs=[ANY] * 7 + [pl.BlockSpec(memory_space=pltpu.VMEM)] * 2,
        out_specs=pl.BlockSpec(memory_space=pltpu.VMEM),
        scratch_shapes=[
            pltpu.VMEM((n, cap, width), BF16),
            pltpu.VMEM((8,) + stream.shape, BF16),
            pltpu.VMEM((8,) + stream.shape, BF16),
            pltpu.VMEM((n, 4, cap, width), BF16),
            pltpu.VMEM((n, 4, cap, width), BF16),
            pltpu.VMEM((n, 2, cap, width), BF16),
            pltpu.VMEM((n, cap, width), BF16),
            pltpu.VMEM((n, cap, width), BF16),
            pltpu.VMEM((n, cap, width), BF16),
            pltpu.VMEM(wg.shape, BF16),
            pltpu.VMEM(wu.shape, BF16),
            pltpu.VMEM(wd.shape, BF16),
            dma((n,)),
            dma((n,)),
            dma((n,)),
            dma((n,)),
            dma((n, 2)),
            dma((n, 2)),
            dma((n,)),
            dma((n,)),
            dma((n,)),
            dma((n,)),
            dma((n,)),
            dma((n,)),
            dma((8,)),
            dma((8,)),
            dma((4,)),
        ],
        compiler_params=params(3),
        name="experts",
    )(rows, *own, *moved, weights, stream)


def body(
    queries,
    keys,
    values,
    segments,
    residual,
    out_weight,
    norm_gain,
    router,
    routes,
    gate_weight,
    up_weight,
    down_weight,
):
    tok, width = residual.shape
    own = (gate_weight[0, 0].T, up_weight[0, 0].T, down_weight[0, 0])
    padded = jnp.pad(routes, ((0, 0), (0, 128 - routes.shape[1])), constant_values=-1)
    stream, rows, weights, *moved = front(
        queries,
        keys,
        values,
        segments,
        out_weight,
        residual,
        norm_gain,
        padded,
        router.T,
        own,
    )
    return experts(rows.reshape(8, 8 * CAP, width), own, moved, weights, stream)


def solution(mesh):
    placed = (
        P("ctx", "ep"),
        P("ctx", "ep"),
        P("ctx", "ep"),
        P(),
        P(("ctx", "ep"), None),
        P("ep", None),
        P(),
        P(),
        P(("ctx", "ep"), None),
        P("ep", "ctx", None, None),
        P("ep", "ctx", None, None),
        P("ep", "ctx", None, None),
    )
    return jax.shard_map(
        body, mesh=mesh, in_specs=placed, out_specs=P(("ctx", "ep"), None), check_vma=False
    )
```
